32 devices in a mesh: mem: 4 (over y, x), col: 8 (over z, core).
Axes of the slice: x: 2, y: 2, z: 4, core: 2. Of those that a mesh axis runs over, the one named last changes fastest.
Arguments:
- ensemble: bfloat16 [256, 3, 128, 1024], P('mem', None, None, 'col'), may hold values from -6 to 6
- increment: bfloat16 [3, 128, 1024], P(None, 'mem', 'col'), may hold values from -6 to 6
- vert_root: bfloat16 [3, 128, 128], replicated, may hold values from -1 to 2, as said below
- tiles: bfloat16 [8, 8, 128, 128], replicated, may hold values from -2 to 3, as said below
- tile_col: int32 [8, 8], replicated, may hold values from 0 to 7, as said below
- level_reach: int32 [128], replicated, may hold values from 2 to 8, as said below
Outputs:
- covaried: bfloat16 [3, 128, 1024], P(None, 'mem', 'col')
The draws below stay inside these ranges and needn't reach their ends.
Inputs may be any that keep to these rules, and one draw needn't show every extreme that they name: `vert_root`: each variable's matrix is the identity plus bounded noise. `tiles`: slot 0 of block row r is the identity plus bounded noise; the other slots are bounded noise. `tile_col`: each row r names K distinct column blocks; slot 0 names r itself. `level_reach`: level 0 uses 2 slots and the top level uses all 8; the count mostly rises with the level.
All inputs are finite; a program needn't handle non-finite values.
Results may differ from the reference program's by a relative error of at most 0.012.
Values may be sent and summed in bfloat16 or wider, within the bound.
A program may use at most 128 MiB of HBM per device.

```python
import jax
import jax.numpy as jnp
from jax import lax

NV = 3
NL = 128
TILE = 128
K = 8
MEMBERS = 256
BLOCKS = 8
NC = 1024


def draw_vert_root(key, part):
    noise = jnp.clip(jax.random.normal(key, (NV, NL, NL), jnp.float32), -6.0, 6.0)
    eye = jnp.eye(NL, dtype=jnp.float32)
    return (eye[None] + 0.5 * noise / jnp.sqrt(NL * 1.0)).astype(jnp.bfloat16)


def draw_tiles(key, part):
    noise = jnp.clip(jax.random.normal(key, (BLOCKS, K, TILE, TILE), jnp.float32), -6.0, 6.0)
    scaled = noise / jnp.sqrt(TILE * K * 1.0)
    first = (jnp.arange(K) == 0).astype(jnp.float32)
    eye = jnp.eye(TILE, dtype=jnp.float32)
    return (scaled + first[None, :, None, None] * eye[None, None]).astype(jnp.bfloat16)


def draw_tile_col(key, part):

    def one_row(index):
        shuffled = jax.random.permutation(jax.random.fold_in(key, index), BLOCKS - 1) + 1
        offsets = jnp.concatenate([jnp.zeros((1,), jnp.int32), shuffled[:K - 1].astype(jnp.int32)])
        return (index + offsets) % BLOCKS
    return jax.vmap(one_row)(jnp.arange(BLOCKS, dtype=jnp.int32)).astype(jnp.int32)


def draw_level_reach(key, part):
    levels = jnp.arange(NL, dtype=jnp.int32)
    base = 2 + (K - 2) * levels // (NL - 1)
    jitter = jax.random.randint(key, (NL,), -1, 1).astype(jnp.int32)
    reach = jnp.clip(base + jitter, 2, K)
    return jnp.where(levels == NL - 1, K, reach).astype(jnp.int32)


def shard_levels(own_key, extent, pieces, low, high):
    factor_of, own = 1.0, jax.random.fold_in(own_key, 6)
    for position, parts in pieces:
        heights = jnp.exp(jax.random.uniform(jax.random.fold_in(own, position), (parts,), jnp.float32, low / len(pieces), high / len(pieces)))
        factor_of = factor_of * jnp.repeat(heights, extent[position] // parts).reshape([-1 if axis == position else 1 for axis in range(len(extent))])
    return factor_of


def centred(stream_key, extent, spread, limit, pieces=(), kind=jnp.bfloat16):
    entries = spread * jax.random.normal(stream_key, extent, jnp.float32)
    if pieces:
        entries = entries * shard_levels(stream_key, extent, pieces, -0.22, 0.18)
    return jnp.clip(entries, -limit, limit).astype(kind)


def setup_inputs(seed: int = 0) -> dict:
    splits = jax.random.split(jax.random.key(seed), 7)
    return {
        "ensemble": centred(splits[0], (MEMBERS, NV, NL, NC), 1.0, 6.0, ((0, 4), (3, 8))),
        "increment": centred(splits[1], (NV, NL, NC), 1.0, 6.0, ((1, 4), (2, 8))),
        "vert_root": draw_vert_root(jax.random.fold_in(splits[6], 71), 0),
        "tiles": draw_tiles(jax.random.fold_in(splits[6], 71), 0),
        "tile_col": draw_tile_col(jax.random.fold_in(splits[6], 71), 0),
        "level_reach": draw_level_reach(jax.random.fold_in(splits[6], 71), 0),
    }


def reference(ensemble, increment, vert_root, tiles, tile_col, level_reach):
    vertical_factor = vert_root.astype(jnp.float32)
    slots = jnp.arange(K, dtype=jnp.int32)
    active = (slots[None, :] < level_reach[:, None]).astype(jnp.float32)
    tile_f = tiles.astype(jnp.float32)
    incr_f = increment.astype(jnp.float32)

    def member_step(total, member):
        member_f = member.astype(jnp.float32)
        weighted_increment = (member_f * incr_f).astype(jnp.bfloat16)
        lifted_increment = jnp.einsum('qzw,qzn->qwn', vertical_factor, weighted_increment.astype(jnp.float32)).astype(jnp.bfloat16)
        grid = lifted_increment.astype(jnp.float32).reshape(NV, NL, BLOCKS, TILE)
        spread_increment = jnp.zeros((NV, NL, BLOCKS, TILE), jnp.float32)
        for slot in range(K):
            picked = jnp.take(grid, tile_col[:, slot], axis=2)
            term = jnp.einsum('vlbi,bij->vlbj', picked, tile_f[:, slot])
            spread_increment = spread_increment + term * active[:, slot][None, :, None, None]
        spread_increment = spread_increment.reshape(NV, NL, NC).astype(jnp.bfloat16)
        lowered_increment = jnp.einsum('duw,dws->dus', vertical_factor, spread_increment.astype(jnp.float32))
        return total + member_f * lowered_increment, None

    total, _ = lax.scan(member_step, jnp.zeros((NV, NL, NC), jnp.float32), ensemble)
    return (total / (MEMBERS - 1)).astype(jnp.bfloat16)
```

```python
import functools

import jax
import jax.numpy as jnp
from jax import lax
from jax.experimental import pallas as pl
from jax.experimental.pallas import tpu as pltpu
from jax.sharding import PartitionSpec as P


def kernel(
    n_mem, n_col, halves, scale,
    slot_block, ens, inc, root, root_t, tiles, active, out,
    recv, incr, grid, picked, total, part_out, part_in, line_out, line_in,
    send_sem, recv_sem, own_sem, inc_send, inc_recv, inc2_send, inc2_recv,
    part_send, part_recv, line_send, line_recv,
):
    mem, col = lax.axis_index("mem"), lax.axis_index("col")
    variables, levels, width = ens.shape[1], ens.shape[2], ens.shape[3]
    per_device = ens.shape[0] // n_col
    group = per_device // halves
    quarter = levels // n_mem
    slots = active.shape[0]
    chunks = variables * halves

    def col_peer(step):
        return lax.rem(col + step, n_col)

    def mem_peer(step):
        return lax.rem(mem + step, n_mem)

    def each(low, high, body):
        def step(index, carry):
            body(index)
            return carry
        lax.fori_loop(low, high, step, 0)

    def remote(src, dst, send, receive, peer):
        return pltpu.make_async_remote_copy(
            src_ref=src, dst_ref=dst, send_sem=send, recv_sem=receive,
            device_id=peer, device_id_type=pl.DeviceIdType.MESH,
        )

    def members_of(owner, chunk):
        first = owner * per_device + lax.rem(chunk, halves) * group
        return ens.at[pl.ds(first, group), chunk // halves]

    def member_copy(chunk, step):
        peer = col_peer(step)
        return remote(
            members_of(peer, chunk), recv.at[chunk, col],
            send_sem.at[chunk, peer], recv_sem.at[chunk, col], {"col": peer},
        )

    def member_arrival(chunk, step):
        peer = col_peer(step)
        return remote(
            members_of(peer, chunk), recv.at[chunk, peer],
            send_sem.at[chunk, peer], recv_sem.at[chunk, peer], {"col": peer},
        )

    def own_copy(chunk):
        return pltpu.make_async_copy(
            members_of(col, chunk), recv.at[chunk, col], own_sem.at[chunk]
        )

    def send_chunk(chunk):
        own_copy(chunk).start()
        each(1, n_col, lambda step: member_copy(chunk, step).start())

    def inc_copy(step):
        peer = col_peer(step)
        return remote(inc, incr.at[mem, col], inc_send.at[peer], inc_recv.at[col], {"col": peer})

    def inc_arrival(step):
        peer = col_peer(step)
        return remote(inc, incr.at[mem, peer], inc_send.at[peer], inc_recv.at[peer], {"col": peer})

    def inc2_copy(step):
        peer = mem_peer(step)
        return remote(
            incr.at[mem], incr.at[mem], inc2_send.at[peer], inc2_recv.at[mem], {"mem": peer}
        )

    def inc2_arrival(step):
        peer = mem_peer(step)
        return remote(
            incr.at[peer], incr.at[peer], inc2_send.at[peer], inc2_recv.at[peer], {"mem": peer}
        )

    def part_copy(v, step):
        peer = mem_peer(step)
        return remote(
            part_out.at[v, peer], part_in.at[v, mem],
            part_send.at[v, peer], part_recv.at[v, mem], {"mem": peer},
        )

    def part_arrival(v, step):
        peer = mem_peer(step)
        return remote(
            part_out.at[v, peer], part_in.at[v, peer],
            part_send.at[v, peer], part_recv.at[v, peer], {"mem": peer},
        )

    def line_copy(v, step):
        peer = col_peer(step)
        return remote(
            line_out.at[v, peer], line_in.at[v, col],
            line_send.at[v, peer], line_recv.at[v, col], {"col": peer},
        )

    def line_arrival(v, step):
        peer = col_peer(step)
        return remote(
            line_out.at[v, peer], line_in.at[v, peer],
            line_send.at[v, peer], line_recv.at[v, peer], {"col": peer},
        )

    barrier = pltpu.get_barrier_semaphore()
    for step in range(1, n_col):
        pl.semaphore_signal(
            barrier, inc=1, device_id={"col": col_peer(step)},
            device_id_type=pl.DeviceIdType.MESH,
        )
    for step in range(1, n_mem):
        pl.semaphore_signal(
            barrier, inc=1, device_id={"mem": mem_peer(step)},
            device_id_type=pl.DeviceIdType.MESH,
        )
    pl.semaphore_wait(barrier, n_col + n_mem - 2)

    each(1, n_col, lambda step: inc_copy(step).start())
    send_chunk(0)
    if chunks > 1:
        send_chunk(1)
    incr[mem, col] = inc[...]
    each(1, n_col, lambda step: inc_arrival(step).wait_recv())
    each(1, n_mem, lambda step: inc2_copy(step).start())
    each(1, n_mem, lambda step: inc2_arrival(step).wait_recv())

    def finish_levels(v):
        each(1, n_mem, lambda step: part_arrival(v, step).wait_recv())

        def block(b):
            summed = total[v, mem, b]
            for step in range(1, n_mem):
                summed += part_in[v, mem_peer(step), b].astype(jnp.float32)
            total[v, mem, b] = summed
            line_out[v, b] = summed.astype(jnp.bfloat16)

        each(0, n_col, block)
        each(1, n_col, lambda step: line_copy(v, step).start())

    def chunk_step(chunk):
        v, half = chunk // halves, lax.rem(chunk, halves)
        own_copy(chunk).wait()
        each(1, n_col, lambda step: member_arrival(chunk, step).wait_recv())

        @pl.when(chunk + 2 < chunks)
        def _():
            send_chunk(chunk + 2)

        def lift(b):
            field = jnp.concatenate([incr[p, b, v] for p in range(n_mem)], 0).astype(jnp.float32)
            weighted = jnp.concatenate(
                [
                    (recv[chunk, b, i].astype(jnp.float32) * field).astype(jnp.bfloat16)
                    for i in range(group)
                ],
                1,
            )
            lifted = jnp.dot(
                root_t[v], weighted, preferred_element_type=jnp.float32
            ).astype(jnp.bfloat16)
            for i in range(group):
                grid[b, i] = lifted[:, i * width:(i + 1) * width]

        each(0, n_col, lift)

        def spread(r):
            for s in range(slots):
                source = grid[slot_block[r, s]]
                picked[:, :, s * width:(s + 1) * width] = source * active[s][None]
            spread_rows = jnp.dot(
                picked[...].reshape(group * levels, slots * width), tiles[r],
                preferred_element_type=jnp.float32,
            ).astype(jnp.bfloat16)
            side = jnp.concatenate(
                [spread_rows[i * levels:(i + 1) * levels] for i in range(group)], 1
            )
            lowered = jnp.dot(root[v], side, preferred_element_type=jnp.float32)
            summed = recv[chunk, r, 0].astype(jnp.float32) * lowered[:, :width]
            for i in range(1, group):
                summed += (
                    recv[chunk, r, i].astype(jnp.float32) * lowered[:, i * width:(i + 1) * width]
                )
            for p in range(n_mem):
                piece = summed[p * quarter:(p + 1) * quarter]

                @pl.when(half == 0)
                def _():
                    total[v, p, r] = piece

                @pl.when(half != 0)
                def _():
                    total[v, p, r] += piece

                @pl.when(half == halves - 1)
                def _():
                    part_out[v, p, r] = total[v, p, r].astype(jnp.bfloat16)

        each(0, n_col, spread)

        @pl.when(half == halves - 1)
        def _():
            each(1, n_mem, lambda step: part_copy(v, step).start())

        @pl.when((half == 0) & (v > 0))
        def _():
            finish_levels(v - 1)

    each(0, chunks, chunk_step)
    finish_levels(variables - 1)

    for v in range(variables):
        each(1, n_col, lambda step: line_arrival(v, step).wait_recv())
        summed = total[v, mem, col]
        for step in range(1, n_col):
            summed += line_in[v, col_peer(step)].astype(jnp.float32)
        out[v] = (summed / scale).astype(out.dtype)

    each(1, n_col, lambda step: inc_copy(step).wait_send())
    each(1, n_mem, lambda step: inc2_copy(step).wait_send())
    each(0, chunks, lambda chunk: each(
        1, n_col, lambda step: member_copy(chunk, step).wait_send()))
    each(0, variables, lambda v: each(
        1, n_mem, lambda step: part_copy(v, step).wait_send()))
    each(0, variables, lambda v: each(
        1, n_col, lambda step: line_copy(v, step).wait_send()))


def on_device(ensemble, increment, vert_root, tiles, tile_col, level_reach):
    n_mem, n_col = lax.axis_size("mem"), lax.axis_size("col")
    members, variables, levels, width = ensemble.shape
    n_blocks, slots = tiles.shape[:2]
    per_device = members // n_col
    halves = 2 if per_device % 2 == 0 else 1
    group = per_device // halves
    chunks = variables * halves
    quarter = levels // n_mem
    active = jnp.broadcast_to(
        (jnp.arange(slots, dtype=jnp.int32)[:, None] < level_reach[None])[:, :, None],
        (slots, levels, width),
    ).astype(jnp.bfloat16)
    dma = pltpu.SemaphoreType.DMA
    vmem = pl.BlockSpec(memory_space=pltpu.VMEM)
    bf16 = jnp.bfloat16
    return pl.pallas_call(
        functools.partial(kernel, n_mem, n_col, halves, float(members * n_mem - 1)),
        out_shape=jax.ShapeDtypeStruct(increment.shape, bf16),
        in_specs=[
            pl.BlockSpec(memory_space=pltpu.SMEM),
            pl.BlockSpec(memory_space=pl.ANY),
            vmem, vmem, vmem, vmem, vmem,
        ],
        out_specs=vmem,
        scratch_shapes=[
            pltpu.VMEM((chunks, n_col, group, levels, width), bf16),
            pltpu.VMEM((n_mem, n_col, variables, quarter, width), bf16),
            pltpu.VMEM((n_col, group, levels, width), bf16),
            pltpu.VMEM((group, levels, slots * width), bf16),
            pltpu.VMEM((variables, n_mem, n_col, quarter, width), jnp.float32),
            pltpu.VMEM((variables, n_mem, n_col, quarter, width), bf16),
            pltpu.VMEM((variables, n_mem, n_col, quarter, width), bf16),
            pltpu.VMEM((variables, n_col, quarter, width), bf16),
            pltpu.VMEM((variables, n_col, quarter, width), bf16),
            dma((chunks, n_col)),
            dma((chunks, n_col)),
            dma((chunks,)),
            dma((n_col,)),
            dma((n_col,)),
            dma((n_mem,)),
            dma((n_mem,)),
            dma((variables, n_mem)),
            dma((variables, n_mem)),
            dma((variables, n_col)),
            dma((variables, n_col)),
        ],
        compiler_params=pltpu.CompilerParams(
            collective_id=0, has_side_effects=True, vmem_limit_bytes=56 * 1024 * 1024
        ),
        name="localized_covariance",
    )(
        tile_col, ensemble, increment, vert_root, jnp.swapaxes(vert_root, 1, 2),
        tiles.reshape(n_blocks, slots * width, width), active,
    )


def solution(mesh):
    placed = (P("mem", None, None, "col"), P(None, "mem", "col"), P(), P(), P(), P())
    return jax.shard_map(
        on_device, mesh=mesh, in_specs=placed, out_specs=P(None, "mem", "col"), check_vma=False
    )
```

```python
import functools

import jax
import jax.numpy as jnp
from jax import lax
from jax.experimental import pallas as pl
from jax.experimental.pallas import tpu as pltpu
from jax.sharding import PartitionSpec as P


def kernel(
    n_mem, n_col, halves, scale,
    slot_block, ens, inc, root_in, tiles_in, reach, out,
    root, root_t, tiles, active, load_sem, recv, incr, grid, picked, total, part_out, part_in, line_out, line_in,
    send_sem, recv_sem, own_sem, inc_send, inc_recv, inc2_send, inc2_recv,
    part_send, part_recv, line_send, line_recv,
):
    mem, col = lax.axis_index("mem"), lax.axis_index("col")
    variables, levels, width = ens.shape[1], ens.shape[2], ens.shape[3]
    per_device = ens.shape[0] // n_col
    group = per_device // halves
    quarter = levels // n_mem
    slots = active.shape[0]
    chunks = variables * halves
    ahead = min(4, chunks)

    def col_peer(step):
        return lax.rem(col + step, n_col)

    def mem_peer(step):
        return lax.rem(mem + step, n_mem)

    def each(low, high, body):
        def step(index, carry):
            body(index)
            return carry
        lax.fori_loop(low, high, step, 0)

    def remote(src, dst, send, receive, peer):
        return pltpu.make_async_remote_copy(
            src_ref=src, dst_ref=dst, send_sem=send, recv_sem=receive,
            device_id=peer, device_id_type=pl.DeviceIdType.MESH,
        )

    def members_of(owner, chunk):
        first = owner * per_device + lax.rem(chunk, halves) * group
        return ens.at[pl.ds(first, group), chunk // halves]

    def member_copy(chunk, step):
        peer = col_peer(step)
        return remote(
            members_of(peer, chunk), recv.at[chunk, col],
            send_sem.at[chunk, peer], recv_sem.at[chunk, col], {"col": peer},
        )

    def member_arrival(chunk, step):
        peer = col_peer(step)
        return remote(
            members_of(peer, chunk), recv.at[chunk, peer],
            send_sem.at[chunk, peer], recv_sem.at[chunk, peer], {"col": peer},
        )

    def own_copy(chunk):
        return pltpu.make_async_copy(
            members_of(col, chunk), recv.at[chunk, col], own_sem.at[chunk]
        )

    def send_chunk(chunk):
        own_copy(chunk).start()
        each(1, n_col, lambda step: member_copy(chunk, step).start())

    def inc_copy(step):
        peer = col_peer(step)
        return remote(inc, incr.at[mem, col], inc_send.at[peer], inc_recv.at[col], {"col": peer})

    def inc_arrival(step):
        peer = col_peer(step)
        return remote(inc, incr.at[mem, peer], inc_send.at[peer], inc_recv.at[peer], {"col": peer})

    def inc2_copy(step):
        peer = mem_peer(step)
        return remote(
            incr.at[mem], incr.at[mem], inc2_send.at[peer], inc2_recv.at[mem], {"mem": peer}
        )

    def inc2_arrival(step):
        peer = mem_peer(step)
        return remote(
            incr.at[peer], incr.at[peer], inc2_send.at[peer], inc2_recv.at[peer], {"mem": peer}
        )

    def part_copy(v, step):
        peer = mem_peer(step)
        return remote(
            part_out.at[v, peer], part_in.at[v, mem],
            part_send.at[v, peer], part_recv.at[v, mem], {"mem": peer},
        )

    def part_arrival(v, step):
        peer = mem_peer(step)
        return remote(
            part_out.at[v, peer], part_in.at[v, peer],
            part_send.at[v, peer], part_recv.at[v, peer], {"mem": peer},
        )

    def line_copy(v, step):
        peer = col_peer(step)
        return remote(
            line_out.at[v, peer], line_in.at[v, col],
            line_send.at[v, peer], line_recv.at[v, col], {"col": peer},
        )

    def line_arrival(v, step):
        peer = col_peer(step)
        return remote(
            line_out.at[v, peer], line_in.at[v, peer],
            line_send.at[v, peer], line_recv.at[v, peer], {"col": peer},
        )

    root_load = pltpu.make_async_copy(root_in, root, load_sem.at[0])
    tiles_load = pltpu.make_async_copy(tiles_in, tiles, load_sem.at[1])
    root_load.start()
    tiles_load.start()

    barrier = pltpu.get_barrier_semaphore()
    for step in range(1, n_col):
        pl.semaphore_signal(
            barrier, inc=1, device_id={"col": col_peer(step)},
            device_id_type=pl.DeviceIdType.MESH,
        )
    for step in range(1, n_mem):
        pl.semaphore_signal(
            barrier, inc=1, device_id={"mem": mem_peer(step)},
            device_id_type=pl.DeviceIdType.MESH,
        )
    pl.semaphore_wait(barrier, n_col + n_mem - 2)

    each(1, n_col, lambda step: inc_copy(step).start())
    each(0, ahead, send_chunk)
    incr[mem, col] = inc[...]
    reach_rows = jnp.broadcast_to(reach[...].astype(jnp.float32), (width, levels)).T
    for s in range(slots):
        active[s] = jnp.where(reach_rows > float(s), 1.0, 0.0).astype(jnp.bfloat16)
    root_load.wait()
    for v in range(variables):
        root_t[v] = root[v].astype(jnp.float32).T.astype(jnp.bfloat16)

    def clear(v):
        for p in range(n_mem):
            total[v, p] = jnp.zeros(total.shape[2:], jnp.float32)

    each(0, variables, clear)
    tiles_load.wait()
    each(1, n_col, lambda step: inc_arrival(step).wait_recv())
    each(1, n_mem, lambda step: inc2_copy(step).start())
    each(1, n_mem, lambda step: inc2_arrival(step).wait_recv())

    def finish_levels(v):
        each(1, n_mem, lambda step: part_arrival(v, step).wait_recv())

        def block(b):
            summed = total[v, mem, b]
            for step in range(1, n_mem):
                summed += part_in[v, mem_peer(step), b].astype(jnp.float32)
            total[v, mem, b] = summed
            line_out[v, b] = summed.astype(jnp.bfloat16)

        each(0, n_col, block)
        each(1, n_col, lambda step: line_copy(v, step).start())

    def chunk_step(chunk):
        v, half = chunk // halves, lax.rem(chunk, halves)
        own_copy(chunk).wait()
        each(1, n_col, lambda step: member_arrival(chunk, step).wait_recv())

        @pl.when(chunk + ahead < chunks)
        def _():
            send_chunk(chunk + ahead)

        def lift(b):
            field = jnp.concatenate([incr[p, b, v] for p in range(n_mem)], 0).astype(jnp.float32)
            weighted = jnp.concatenate(
                [
                    (recv[chunk, b, i].astype(jnp.float32) * field).astype(jnp.bfloat16)
                    for i in range(group)
                ],
                1,
            )
            lifted = jnp.dot(
                root_t[v], weighted, preferred_element_type=jnp.float32
            ).astype(jnp.bfloat16)
            for i in range(group):
                grid[b, i] = lifted[:, i * width:(i + 1) * width]

        each(0, n_col, lift)

        def spread(r):
            for s in range(slots):
                source = grid[slot_block[r, s]]
                picked[:, :, s * width:(s + 1) * width] = source * active[s][None]
            spread_rows = jnp.dot(
                picked[...].reshape(group * levels, slots * width), tiles[r],
                preferred_element_type=jnp.float32,
            ).astype(jnp.bfloat16)
            side = jnp.concatenate(
                [spread_rows[i * levels:(i + 1) * levels] for i in range(group)], 1
            )
            lowered = jnp.dot(root[v], side, preferred_element_type=jnp.float32)
            summed = recv[chunk, r, 0].astype(jnp.float32) * lowered[:, :width]
            for i in range(1, group):
                summed += (
                    recv[chunk, r, i].astype(jnp.float32) * lowered[:, i * width:(i + 1) * width]
                )
            for p in range(n_mem):
                total[v, p, r] += summed[p * quarter:(p + 1) * quarter]

            @pl.when(half == halves - 1)
            def _():
                for p in range(n_mem):
                    part_out[v, p, r] = total[v, p, r].astype(jnp.bfloat16)

        each(0, n_col, spread)

        @pl.when(half == halves - 1)
        def _():
            each(1, n_mem, lambda step: part_copy(v, step).start())

        @pl.when((half == 0) & (v > 0))
        def _():
            finish_levels(v - 1)

    each(0, chunks, chunk_step)
    finish_levels(variables - 1)

    for v in range(variables):
        each(1, n_col, lambda step: line_arrival(v, step).wait_recv())
        summed = total[v, mem, col]
        for step in range(1, n_col):
            summed += line_in[v, col_peer(step)].astype(jnp.float32)
        out[v] = (summed / scale).astype(out.dtype)

    each(1, n_col, lambda step: inc_copy(step).wait_send())
    each(1, n_mem, lambda step: inc2_copy(step).wait_send())
    each(0, chunks, lambda chunk: each(
        1, n_col, lambda step: member_copy(chunk, step).wait_send()))
    each(0, variables, lambda v: each(
        1, n_mem, lambda step: part_copy(v, step).wait_send()))
    each(0, variables, lambda v: each(
        1, n_col, lambda step: line_copy(v, step).wait_send()))


def on_device(ensemble, increment, vert_root, tiles, tile_col, level_reach):
    n_mem, n_col = lax.axis_size("mem"), lax.axis_size("col")
    members, variables, levels, width = ensemble.shape
    n_blocks, slots = tiles.shape[:2]
    per_device = members // n_col
    halves = per_device // 2 if per_device % 4 == 0 else 2 - per_device % 2
    group = per_device // halves
    chunks = variables * halves
    quarter = levels // n_mem
    dma = pltpu.SemaphoreType.DMA
    vmem = pl.BlockSpec(memory_space=pltpu.VMEM)
    bf16 = jnp.bfloat16
    return pl.pallas_call(
        functools.partial(kernel, n_mem, n_col, halves, float(members * n_mem - 1)),
        out_shape=jax.ShapeDtypeStruct(increment.shape, bf16),
        in_specs=[
            pl.BlockSpec(memory_space=pltpu.SMEM),
            pl.BlockSpec(memory_space=pl.ANY),
            vmem, pl.BlockSpec(memory_space=pl.ANY), pl.BlockSpec(memory_space=pl.ANY), vmem,
        ],
        out_specs=vmem,
        scratch_shapes=[
            pltpu.VMEM(vert_root.shape, bf16),
            pltpu.VMEM(vert_root.shape, bf16),
            pltpu.VMEM((n_blocks, slots * width, width), bf16),
            pltpu.VMEM((slots, levels, width), bf16),
            dma((2,)),
            pltpu.VMEM((chunks, n_col, group, levels, width), bf16),
            pltpu.VMEM((n_mem, n_col, variables, quarter, width), bf16),
            pltpu.VMEM((n_col, group, levels, width), bf16),
            pltpu.VMEM((group, levels, slots * width), bf16),
            pltpu.VMEM((variables, n_mem, n_col, quarter, width), jnp.float32),
            pltpu.VMEM((variables, n_mem, n_col, quarter, width), bf16),
            pltpu.VMEM((variables, n_mem, n_col, quarter, width), bf16),
            pltpu.VMEM((variables, n_col, quarter, width), bf16),
            pltpu.VMEM((variables, n_col, quarter, width), bf16),
            dma((chunks, n_col)),
            dma((chunks, n_col)),
            dma((chunks,)),
            dma((n_col,)),
            dma((n_col,)),
            dma((n_mem,)),
            dma((n_mem,)),
            dma((variables, n_mem)),
            dma((variables, n_mem)),
            dma((variables, n_col)),
            dma((variables, n_col)),
        ],
        compiler_params=pltpu.CompilerParams(
            collective_id=0, has_side_effects=True, vmem_limit_bytes=56 * 1024 * 1024
        ),
        name="localized_covariance",
    )(
        tile_col, ensemble, increment, vert_root,
        tiles.reshape(n_blocks, slots * width, width), level_reach.reshape(1, levels),
    )


def solution(mesh):
    placed = (P("mem", None, None, "col"), P(None, "mem", "col"), P(), P(), P(), P())
    return jax.shard_map(
        on_device, mesh=mesh, in_specs=placed, out_specs=P(None, "mem", "col"), check_vma=False
    )
```

```python
import functools

import jax
import jax.numpy as jnp
from jax import lax
from jax.experimental import pallas as pl
from jax.experimental.pallas import tpu as pltpu
from jax.sharding import PartitionSpec as P


def kernel(
    n_mem, n_col, halves, scale,
    slot_block, ens, inc, root_in, tiles_in, reach, out,
    root, root_t, tiles, active, load_sem, recv, incr, grid, total, part_out, part_in, line_out, line_in,
    send_sem, recv_sem, own_sem, inc_send, inc_recv, inc2_send, inc2_recv,
    part_send, part_recv, line_send, line_recv,
):
    mem, col = lax.axis_index("mem"), lax.axis_index("col")
    variables, levels, width = ens.shape[1], ens.shape[2], ens.shape[3]
    per_device = ens.shape[0] // n_col
    group = per_device // halves
    quarter = levels // n_mem
    slots = active.shape[0]
    chunks = variables * halves
    ahead = min(3, chunks)
    side_by_side = 4 if n_col % 4 == 0 else 1

    def col_peer(step):
        return lax.rem(col + step, n_col)

    def mem_peer(step):
        return lax.rem(mem + step, n_mem)

    def each(low, high, body):
        def step(index, carry):
            body(index)
            return carry
        lax.fori_loop(low, high, step, 0)

    def together(body):
        def step(index):
            for k in range(side_by_side):
                body(index * side_by_side + k)
        each(0, n_col // side_by_side, step)

    def remote(src, dst, send, receive, peer):
        return pltpu.make_async_remote_copy(
            src_ref=src, dst_ref=dst, send_sem=send, recv_sem=receive,
            device_id=peer, device_id_type=pl.DeviceIdType.MESH,
        )

    def far_first(k):
        return n_col // 2 + (k // 2) * (1 - 2 * lax.rem(k, 2))

    def members_of(owner, chunk):
        first = owner * per_device + lax.rem(chunk, halves) * group
        return ens.at[pl.ds(first, group), chunk // halves]

    def member_copy(chunk, step):
        peer = col_peer(step)
        return remote(
            members_of(peer, chunk), recv.at[chunk, col],
            send_sem.at[chunk, peer], recv_sem.at[chunk, col], {"col": peer},
        )

    def member_arrival(chunk, step):
        peer = col_peer(step)
        return remote(
            members_of(peer, chunk), recv.at[chunk, peer],
            send_sem.at[chunk, peer], recv_sem.at[chunk, peer], {"col": peer},
        )

    def own_copy(chunk):
        return pltpu.make_async_copy(
            members_of(col, chunk), recv.at[chunk, col], own_sem.at[chunk]
        )

    def send_chunk(chunk):
        own_copy(chunk).start()
        each(1, n_col, lambda k: member_copy(chunk, far_first(k)).start())

    def inc_copy(step):
        peer = col_peer(step)
        return remote(inc, incr.at[mem, col], inc_send.at[peer], inc_recv.at[col], {"col": peer})

    def inc_arrival(step):
        peer = col_peer(step)
        return remote(inc, incr.at[mem, peer], inc_send.at[peer], inc_recv.at[peer], {"col": peer})

    def inc2_copy(step):
        peer = mem_peer(step)
        return remote(
            incr.at[mem], incr.at[mem], inc2_send.at[peer], inc2_recv.at[mem], {"mem": peer}
        )

    def inc2_arrival(step):
        peer = mem_peer(step)
        return remote(
            incr.at[peer], incr.at[peer], inc2_send.at[peer], inc2_recv.at[peer], {"mem": peer}
        )

    def part_copy(v, step):
        peer = mem_peer(step)
        return remote(
            part_out.at[v, peer], part_in.at[v, mem],
            part_send.at[v, peer], part_recv.at[v, mem], {"mem": peer},
        )

    def part_arrival(v, step):
        peer = mem_peer(step)
        return remote(
            part_out.at[v, peer], part_in.at[v, peer],
            part_send.at[v, peer], part_recv.at[v, peer], {"mem": peer},
        )

    def line_copy(v, step):
        peer = col_peer(step)
        return remote(
            line_out.at[v, peer], line_in.at[v, col],
            line_send.at[v, peer], line_recv.at[v, col], {"col": peer},
        )

    def line_arrival(v, step):
        peer = col_peer(step)
        return remote(
            line_out.at[v, peer], line_in.at[v, peer],
            line_send.at[v, peer], line_recv.at[v, peer], {"col": peer},
        )

    root_load = pltpu.make_async_copy(root_in, root, load_sem.at[0])
    tiles_load = pltpu.make_async_copy(tiles_in, tiles, load_sem.at[1])
    root_load.start()
    tiles_load.start()

    barrier = pltpu.get_barrier_semaphore()
    for step in range(1, n_col):
        pl.semaphore_signal(
            barrier, inc=1, device_id={"col": col_peer(step)},
            device_id_type=pl.DeviceIdType.MESH,
        )
    for step in range(1, n_mem):
        pl.semaphore_signal(
            barrier, inc=1, device_id={"mem": mem_peer(step)},
            device_id_type=pl.DeviceIdType.MESH,
        )
    pl.semaphore_wait(barrier, n_col + n_mem - 2)

    each(1, n_col, lambda step: inc_copy(step).start())
    each(0, ahead, send_chunk)
    incr[mem, col] = inc[...]
    reach_rows = jnp.broadcast_to(reach[...].astype(jnp.float32), (width, levels)).T
    for s in range(slots):
        active[s] = jnp.where(reach_rows > float(s), 1.0, 0.0).astype(jnp.bfloat16)
    root_load.wait()
    for v in range(variables):
        root_t[v] = root[v].astype(jnp.float32).T.astype(jnp.bfloat16)

    def clear(v):
        for p in range(n_mem):
            total[v, p] = jnp.zeros(total.shape[2:], jnp.float32)

    each(0, variables, clear)
    tiles_load.wait()
    each(1, n_col, lambda step: inc_arrival(step).wait_recv())
    each(1, n_mem, lambda step: inc2_copy(step).start())
    each(1, n_mem, lambda step: inc2_arrival(step).wait_recv())

    def finish_levels(v):
        each(1, n_mem, lambda step: part_arrival(v, step).wait_recv())

        def block(b):
            summed = total[v, mem, b]
            for step in range(1, n_mem):
                summed += part_in[v, mem_peer(step), b].astype(jnp.float32)
            total[v, mem, b] = summed
            line_out[v, b] = summed.astype(jnp.bfloat16)

        each(0, n_col, block)
        each(1, n_col, lambda step: line_copy(v, step).start())

    def chunk_step(chunk):
        v, half = chunk // halves, lax.rem(chunk, halves)
        own_copy(chunk).wait()
        each(1, n_col, lambda step: member_arrival(chunk, step).wait_recv())

        @pl.when(chunk + ahead < chunks)
        def _():
            send_chunk(chunk + ahead)

        def lift(b):
            field = jnp.concatenate([incr[p, b, v] for p in range(n_mem)], 0).astype(jnp.float32)
            weighted = jnp.concatenate(
                [
                    (recv[chunk, b, i].astype(jnp.float32) * field).astype(jnp.bfloat16)
                    for i in range(group)
                ],
                1,
            )
            lifted = jnp.dot(
                root_t[v], weighted, preferred_element_type=jnp.float32
            ).astype(jnp.bfloat16)
            for i in range(group):
                grid[b, i] = lifted[:, i * width:(i + 1) * width]

        together(lift)

        def spread(r):
            picked = jnp.concatenate(
                [grid[slot_block[r, s]] * active[s][None] for s in range(slots)], 2
            )
            spread_rows = jnp.dot(
                picked.reshape(group * levels, slots * width), tiles[r],
                preferred_element_type=jnp.float32,
            ).astype(jnp.bfloat16)
            side = jnp.concatenate(
                [spread_rows[i * levels:(i + 1) * levels] for i in range(group)], 1
            )
            lowered = jnp.dot(root[v], side, preferred_element_type=jnp.float32)
            summed = recv[chunk, r, 0].astype(jnp.float32) * lowered[:, :width]
            for i in range(1, group):
                summed += (
                    recv[chunk, r, i].astype(jnp.float32) * lowered[:, i * width:(i + 1) * width]
                )
            for p in range(n_mem):
                total[v, p, r] += summed[p * quarter:(p + 1) * quarter]

        together(spread)

        @pl.when(half == halves - 1)
        def _():
            for p in range(n_mem):
                part_out[v, p] = total[v, p].astype(jnp.bfloat16)
            each(1, n_mem, lambda step: part_copy(v, step).start())

        @pl.when((half == 0) & (v > 0))
        def _():
            finish_levels(v - 1)

    each(0, chunks, chunk_step)
    finish_levels(variables - 1)

    for v in range(variables):
        each(1, n_col, lambda step: line_arrival(v, step).wait_recv())
        summed = total[v, mem, col]
        for step in range(1, n_col):
            summed += line_in[v, col_peer(step)].astype(jnp.float32)
        out[v] = (summed / scale).astype(out.dtype)

    each(1, n_col, lambda step: inc_copy(step).wait_send())
    each(1, n_mem, lambda step: inc2_copy(step).wait_send())
    each(0, chunks, lambda chunk: each(
        1, n_col, lambda step: member_copy(chunk, step).wait_send()))
    each(0, variables, lambda v: each(
        1, n_mem, lambda step: part_copy(v, step).wait_send()))
    each(0, variables, lambda v: each(
        1, n_col, lambda step: line_copy(v, step).wait_send()))


def on_device(ensemble, increment, vert_root, tiles, tile_col, level_reach):
    n_mem, n_col = lax.axis_size("mem"), lax.axis_size("col")
    members, variables, levels, width = ensemble.shape
    n_blocks, slots = tiles.shape[:2]
    per_device = members // n_col
    halves = per_device // 2 if per_device % 4 == 0 else 2 - per_device % 2
    group = per_device // halves
    chunks = variables * halves
    quarter = levels // n_mem
    dma = pltpu.SemaphoreType.DMA
    vmem = pl.BlockSpec(memory_space=pltpu.VMEM)
    bf16 = jnp.bfloat16
    return pl.pallas_call(
        functools.partial(kernel, n_mem, n_col, halves, float(members * n_mem - 1)),
        out_shape=jax.ShapeDtypeStruct(increment.shape, bf16),
        in_specs=[
            pl.BlockSpec(memory_space=pltpu.SMEM),
            pl.BlockSpec(memory_space=pl.ANY),
            vmem, pl.BlockSpec(memory_space=pl.ANY), pl.BlockSpec(memory_space=pl.ANY), vmem,
        ],
        out_specs=vmem,
        scratch_shapes=[
            pltpu.VMEM(vert_root.shape, bf16),
            pltpu.VMEM(vert_root.shape, bf16),
            pltpu.VMEM((n_blocks, slots * width, width), bf16),
            pltpu.VMEM((slots, levels, width), bf16),
            dma((2,)),
            pltpu.VMEM((chunks, n_col, group, levels, width), bf16),
            pltpu.VMEM((n_mem, n_col, variables, quarter, width), bf16),
            pltpu.VMEM((n_col, group, levels, width), bf16),
            pltpu.VMEM((variables, n_mem, n_col, quarter, width), jnp.float32),
            pltpu.VMEM((variables, n_mem, n_col, quarter, width), bf16),
            pltpu.VMEM((variables, n_mem, n_col, quarter, width), bf16),
            pltpu.VMEM((variables, n_col, quarter, width), bf16),
            pltpu.VMEM((variables, n_col, quarter, width), bf16),
            dma((chunks, n_col)),
            dma((chunks, n_col)),
            dma((chunks,)),
            dma((n_col,)),
            dma((n_col,)),
            dma((n_mem,)),
            dma((n_mem,)),
            dma((variables, n_mem)),
            dma((variables, n_mem)),
            dma((variables, n_col)),
            dma((variables, n_col)),
        ],
        compiler_params=pltpu.CompilerParams(
            collective_id=0, has_side_effects=True, vmem_limit_bytes=56 * 1024 * 1024
        ),
        name="localized_covariance",
    )(
        tile_col, ensemble, increment, vert_root,
        tiles.reshape(n_blocks, slots * width, width), level_reach.reshape(1, levels),
    )


def solution(mesh):
    placed = (P("mem", None, None, "col"), P(None, "mem", "col"), P(), P(), P(), P())
    return jax.shard_map(
        on_device, mesh=mesh, in_specs=placed, out_specs=P(None, "mem", "col"), check_vma=False
    )
```

```python
import functools

import jax
import jax.numpy as jnp
from jax import lax
from jax.experimental import pallas as pl
from jax.experimental.pallas import tpu as pltpu
from jax.sharding import PartitionSpec as P


def kernel(
    n_mem, n_col, halves, scale,
    slot_block, ens, inc, root_in, tiles_in, reach, out,
    root, root_t, tiles, active, load_sem, recv, incr, grid, total, part_out, part_in, line_out, line_in,
    send_sem, recv_sem, own_sem, inc_send, inc_recv, inc2_send, inc2_recv,
    part_send, part_recv, line_send, line_recv,
):
    mem, col = lax.axis_index("mem"), lax.axis_index("col")
    variables, levels, width = ens.shape[1], ens.shape[2], ens.shape[3]
    per_device = ens.shape[0] // n_col
    group = per_device // halves
    quarter = levels // n_mem
    slots = active.shape[0]
    chunks = variables * halves
    ahead = min(6, chunks)
    side_by_side = 4 if n_col % 4 == 0 else 1

    def col_peer(step):
        return lax.rem(col + step, n_col)

    def mem_peer(step):
        return lax.rem(mem + step, n_mem)

    def each(low, high, body):
        def step(index, carry):
            body(index)
            return carry
        lax.fori_loop(low, high, step, 0)

    def together(body):
        def step(index):
            for k in range(side_by_side):
                body(index * side_by_side + k)
        each(0, n_col // side_by_side, step)

    def remote(src, dst, send, receive, peer):
        return pltpu.make_async_remote_copy(
            src_ref=src, dst_ref=dst, send_sem=send, recv_sem=receive,
            device_id=peer, device_id_type=pl.DeviceIdType.MESH,
        )

    def far_first(k):
        return n_col // 2 + (k // 2) * (1 - 2 * lax.rem(k, 2))

    def members_of(owner, chunk):
        first = owner * per_device + lax.rem(chunk, halves) * group
        return ens.at[pl.ds(first, group), chunk // halves]

    def member_copy(chunk, step):
        peer = col_peer(step)
        return remote(
            members_of(peer, chunk), recv.at[chunk, col],
            send_sem.at[chunk, peer], recv_sem.at[chunk, col], {"col": peer},
        )

    def member_arrival(chunk, step):
        peer = col_peer(step)
        return remote(
            members_of(peer, chunk), recv.at[chunk, peer],
            send_sem.at[chunk, peer], recv_sem.at[chunk, peer], {"col": peer},
        )

    def own_copy(chunk):
        return pltpu.make_async_copy(
            members_of(col, chunk), recv.at[chunk, col], own_sem.at[chunk]
        )

    def send_chunk(chunk):
        own_copy(chunk).start()
        each(1, n_col, lambda k: member_copy(chunk, far_first(k)).start())

    def inc_copy(step):
        peer = col_peer(step)
        return remote(inc, incr.at[mem, col], inc_send.at[peer], inc_recv.at[col], {"col": peer})

    def inc_arrival(step):
        peer = col_peer(step)
        return remote(inc, incr.at[mem, peer], inc_send.at[peer], inc_recv.at[peer], {"col": peer})

    def inc2_copy(step):
        peer = mem_peer(step)
        return remote(
            incr.at[mem], incr.at[mem], inc2_send.at[peer], inc2_recv.at[mem], {"mem": peer}
        )

    def inc2_arrival(step):
        peer = mem_peer(step)
        return remote(
            incr.at[peer], incr.at[peer], inc2_send.at[peer], inc2_recv.at[peer], {"mem": peer}
        )

    def part_copy(v, step):
        peer = mem_peer(step)
        return remote(
            part_out.at[v, peer], part_in.at[v, mem],
            part_send.at[v, peer], part_recv.at[v, mem], {"mem": peer},
        )

    def part_arrival(v, step):
        peer = mem_peer(step)
        return remote(
            part_out.at[v, peer], part_in.at[v, peer],
            part_send.at[v, peer], part_recv.at[v, peer], {"mem": peer},
        )

    def line_copy(v, step):
        peer = col_peer(step)
        return remote(
            line_out.at[v, peer], line_in.at[v, col],
            line_send.at[v, peer], line_recv.at[v, col], {"col": peer},
        )

    def line_arrival(v, step):
        peer = col_peer(step)
        return remote(
            line_out.at[v, peer], line_in.at[v, peer],
            line_send.at[v, peer], line_recv.at[v, peer], {"col": peer},
        )

    root_load = pltpu.make_async_copy(root_in, root, load_sem.at[0])
    tiles_load = pltpu.make_async_copy(tiles_in, tiles, load_sem.at[1])
    root_load.start()
    tiles_load.start()

    barrier = pltpu.get_barrier_semaphore()
    for step in range(1, n_col):
        pl.semaphore_signal(
            barrier, inc=1, device_id={"col": col_peer(step)},
            device_id_type=pl.DeviceIdType.MESH,
        )
    for step in range(1, n_mem):
        pl.semaphore_signal(
            barrier, inc=1, device_id={"mem": mem_peer(step)},
            device_id_type=pl.DeviceIdType.MESH,
        )
    pl.semaphore_wait(barrier, n_col + n_mem - 2)

    each(1, n_col, lambda step: inc_copy(step).start())
    each(0, ahead, send_chunk)
    incr[mem, col] = inc[...]
    reach_rows = jnp.broadcast_to(reach[...].astype(jnp.float32), (width, levels)).T
    for s in range(slots):
        active[s] = jnp.where(reach_rows > float(s), 1.0, 0.0).astype(jnp.bfloat16)
    root_load.wait()
    for v in range(variables):
        root_t[v] = root[v].astype(jnp.float32).T.astype(jnp.bfloat16)

    def clear(v):
        for p in range(n_mem):
            total[v, p] = jnp.zeros(total.shape[2:], jnp.float32)

    each(0, variables, clear)
    tiles_load.wait()
    each(1, n_col, lambda step: inc_arrival(step).wait_recv())
    each(1, n_mem, lambda step: inc2_copy(step).start())
    each(1, n_mem, lambda step: inc2_arrival(step).wait_recv())

    def finish_levels(v):
        each(1, n_mem, lambda step: part_arrival(v, step).wait_recv())

        def block(b):
            summed = total[v, mem, b]
            for step in range(1, n_mem):
                summed += part_in[v, mem_peer(step), b].astype(jnp.float32)
            total[v, mem, b] = summed
            line_out[v, b] = summed.astype(jnp.bfloat16)

        each(0, n_col, block)
        each(1, n_col, lambda step: line_copy(v, step).start())

    def chunk_step(chunk):
        v, half = chunk // halves, lax.rem(chunk, halves)
        own_copy(chunk).wait()
        each(1, n_col, lambda step: member_arrival(chunk, step).wait_recv())

        @pl.when(chunk + ahead < chunks)
        def _():
            send_chunk(chunk + ahead)

        def lift(b):
            field = jnp.concatenate([incr[p, b, v] for p in range(n_mem)], 0).astype(jnp.float32)
            weighted = jnp.concatenate(
                [
                    (recv[chunk, b, i].astype(jnp.float32) * field).astype(jnp.bfloat16)
                    for i in range(group)
                ],
                1,
            )
            lifted = jnp.dot(
                root_t[v], weighted, preferred_element_type=jnp.float32
            ).astype(jnp.bfloat16)
            for i in range(group):
                grid[b, i] = lifted[:, i * width:(i + 1) * width]

        together(lift)

        def spread(r):
            picked = jnp.concatenate(
                [grid[slot_block[r, s]] * active[s][None] for s in range(slots)], 2
            )
            spread_rows = jnp.dot(
                picked.reshape(group * levels, slots * width), tiles[r],
                preferred_element_type=jnp.float32,
            ).astype(jnp.bfloat16)
            side = jnp.concatenate(
                [spread_rows[i * levels:(i + 1) * levels] for i in range(group)], 1
            )
            lowered = jnp.dot(root[v], side, preferred_element_type=jnp.float32)
            summed = recv[chunk, r, 0].astype(jnp.float32) * lowered[:, :width]
            for i in range(1, group):
                summed += (
                    recv[chunk, r, i].astype(jnp.float32) * lowered[:, i * width:(i + 1) * width]
                )
            for p in range(n_mem):
                total[v, p, r] += summed[p * quarter:(p + 1) * quarter]

        together(spread)

        @pl.when(half == halves - 1)
        def _():
            for p in range(n_mem):
                part_out[v, p] = total[v, p].astype(jnp.bfloat16)
            each(1, n_mem, lambda step: part_copy(v, step).start())

        @pl.when((half == 0) & (v > 0))
        def _():
            finish_levels(v - 1)

    each(0, chunks, chunk_step)
    finish_levels(variables - 1)

    for v in range(variables):
        each(1, n_col, lambda step: line_arrival(v, step).wait_recv())
        summed = total[v, mem, col]
        for step in range(1, n_col):
            summed += line_in[v, col_peer(step)].astype(jnp.float32)
        out[v] = (summed / scale).astype(out.dtype)

    each(1, n_col, lambda step: inc_copy(step).wait_send())
    each(1, n_mem, lambda step: inc2_copy(step).wait_send())
    each(0, chunks, lambda chunk: each(
        1, n_col, lambda step: member_copy(chunk, step).wait_send()))
    each(0, variables, lambda v: each(
        1, n_mem, lambda step: part_copy(v, step).wait_send()))
    each(0, variables, lambda v: each(
        1, n_col, lambda step: line_copy(v, step).wait_send()))


def on_device(ensemble, increment, vert_root, tiles, tile_col, level_reach):
    n_mem, n_col = lax.axis_size("mem"), lax.axis_size("col")
    members, variables, levels, width = ensemble.shape
    n_blocks, slots = tiles.shape[:2]
    per_device = members // n_col
    halves = per_device
    group = per_device // halves
    chunks = variables * halves
    quarter = levels // n_mem
    dma = pltpu.SemaphoreType.DMA
    vmem = pl.BlockSpec(memory_space=pltpu.VMEM)
    bf16 = jnp.bfloat16
    return pl.pallas_call(
        functools.partial(kernel, n_mem, n_col, halves, float(members * n_mem - 1)),
        out_shape=jax.ShapeDtypeStruct(increment.shape, bf16),
        in_specs=[
            pl.BlockSpec(memory_space=pltpu.SMEM),
            pl.BlockSpec(memory_space=pl.ANY),
            vmem, pl.BlockSpec(memory_space=pl.ANY), pl.BlockSpec(memory_space=pl.ANY), vmem,
        ],
        out_specs=vmem,
        scratch_shapes=[
            pltpu.VMEM(vert_root.shape, bf16),
            pltpu.VMEM(vert_root.shape, bf16),
            pltpu.VMEM((n_blocks, slots * width, width), bf16),
            pltpu.VMEM((slots, levels, width), bf16),
            dma((2,)),
            pltpu.VMEM((chunks, n_col, group, levels, width), bf16),
            pltpu.VMEM((n_mem, n_col, variables, quarter, width), bf16),
            pltpu.VMEM((n_col, group, levels, width), bf16),
            pltpu.VMEM((variables, n_mem, n_col, quarter, width), jnp.float32),
            pltpu.VMEM((variables, n_mem, n_col, quarter, width), bf16),
            pltpu.VMEM((variables, n_mem, n_col, quarter, width), bf16),
            pltpu.VMEM((variables, n_col, quarter, width), bf16),
            pltpu.VMEM((variables, n_col, quarter, width), bf16),
            dma((chunks, n_col)),
            dma((chunks, n_col)),
            dma((chunks,)),
            dma((n_col,)),
            dma((n_col,)),
            dma((n_mem,)),
            dma((n_mem,)),
            dma((variables, n_mem)),
            dma((variables, n_mem)),
            dma((variables, n_col)),
            dma((variables, n_col)),
        ],
        compiler_params=pltpu.CompilerParams(
            collective_id=0, has_side_effects=True, vmem_limit_bytes=56 * 1024 * 1024
        ),
        name="localized_covariance",
    )(
        tile_col, ensemble, increment, vert_root,
        tiles.reshape(n_blocks, slots * width, width), level_reach.reshape(1, levels),
    )


def solution(mesh):
    placed = (P("mem", None, None, "col"), P(None, "mem", "col"), P(), P(), P(), P())
    return jax.shard_map(
        on_device, mesh=mesh, in_specs=placed, out_specs=P(None, "mem", "col"), check_vma=False
    )
```

```python
import functools

import jax
import jax.numpy as jnp
from jax import lax
from jax.experimental import pallas as pl
from jax.experimental.pallas import tpu as pltpu
from jax.sharding import PartitionSpec as P


def kernel(
    n_mem, n_col, halves, scale,
    slot_block, ens, inc, root_in, tiles_in, reach, out,
    root, root_t, tiles, active, load_sem, recv, incr, grid, total, part_out, part_in, line_out, line_in,
    send_sem, recv_sem, own_sem, inc_send, inc_recv, inc2_send, inc2_recv,
    part_send, part_recv, line_send, line_recv,
):
    mem, col = lax.axis_index("mem"), lax.axis_index("col")
    variables, levels, width = ens.shape[1], ens.shape[2], ens.shape[3]
    per_device = ens.shape[0] // n_col
    group = per_device // halves
    quarter = levels // n_mem
    slots = active.shape[0]
    chunks = variables * halves
    ahead = min(3, chunks)
    side_by_side = 4 if n_col % 4 == 0 else 1

    def col_peer(step):
        return lax.rem(col + step, n_col)

    lanes = 2 if n_col % 2 == 0 else 1
    rows, planes = n_col // lanes, n_mem * lanes
    lane, row = lax.rem(col, lanes), col // lanes
    plane = mem * lanes + lane

    def row_peer(step):
        return lax.rem(row + step, rows)

    def plane_peer(step):
        return lax.rem(plane + step, planes)

    def in_row(peer):
        return {"col": peer * lanes + lane}

    def in_plane(peer):
        return {"mem": peer // lanes, "col": row * lanes + lax.rem(peer, lanes)}

    def each(low, high, body):
        def step(index, carry):
            body(index)
            return carry
        lax.fori_loop(low, high, step, 0)

    def together(body):
        def step(index):
            for k in range(side_by_side):
                body(index * side_by_side + k)
        each(0, n_col // side_by_side, step)

    def remote(src, dst, send, receive, peer):
        return pltpu.make_async_remote_copy(
            src_ref=src, dst_ref=dst, send_sem=send, recv_sem=receive,
            device_id=peer, device_id_type=pl.DeviceIdType.MESH,
        )

    def far_first(k):
        return n_col // 2 + (k // 2) * (1 - 2 * lax.rem(k, 2))

    def members_of(owner, chunk):
        first = owner * per_device + lax.rem(chunk, halves) * group
        return ens.at[pl.ds(first, group), chunk // halves]

    def member_copy(chunk, step):
        peer = col_peer(step)
        return remote(
            members_of(peer, chunk), recv.at[chunk, col],
            send_sem.at[chunk, peer], recv_sem.at[chunk, col], {"col": peer},
        )

    def member_arrival(chunk, step):
        peer = col_peer(step)
        return remote(
            members_of(peer, chunk), recv.at[chunk, peer],
            send_sem.at[chunk, peer], recv_sem.at[chunk, peer], {"col": peer},
        )

    def own_copy(chunk):
        return pltpu.make_async_copy(
            members_of(col, chunk), recv.at[chunk, col], own_sem.at[chunk]
        )

    def send_chunk(chunk):
        own_copy(chunk).start()
        each(1, n_col, lambda k: member_copy(chunk, far_first(k)).start())

    def inc_copy(step):
        peer = row_peer(step)
        return remote(inc, incr.at[plane, row], inc_send.at[peer], inc_recv.at[row], in_row(peer))

    def inc_arrival(step):
        peer = row_peer(step)
        return remote(inc, incr.at[plane, peer], inc_send.at[peer], inc_recv.at[peer], in_row(peer))

    def inc2_copy(step):
        peer = plane_peer(step)
        return remote(
            incr.at[plane], incr.at[plane], inc2_send.at[peer], inc2_recv.at[plane],
            in_plane(peer),
        )

    def inc2_arrival(step):
        peer = plane_peer(step)
        return remote(
            incr.at[peer], incr.at[peer], inc2_send.at[peer], inc2_recv.at[peer],
            in_plane(peer),
        )

    def part_copy(v, step):
        peer = plane_peer(step)
        return remote(
            part_out.at[v, peer], part_in.at[v, plane],
            part_send.at[v, peer], part_recv.at[v, plane], in_plane(peer),
        )

    def part_arrival(v, step):
        peer = plane_peer(step)
        return remote(
            part_out.at[v, peer], part_in.at[v, peer],
            part_send.at[v, peer], part_recv.at[v, peer], in_plane(peer),
        )

    def line_copy(v, step):
        peer = row_peer(step)
        return remote(
            line_out.at[v, peer], line_in.at[v, row],
            line_send.at[v, peer], line_recv.at[v, row], in_row(peer),
        )

    def line_arrival(v, step):
        peer = row_peer(step)
        return remote(
            line_out.at[v, peer], line_in.at[v, peer],
            line_send.at[v, peer], line_recv.at[v, peer], in_row(peer),
        )

    root_load = pltpu.make_async_copy(root_in, root, load_sem.at[0])
    tiles_load = pltpu.make_async_copy(tiles_in, tiles, load_sem.at[1])
    root_load.start()
    tiles_load.start()

    barrier = pltpu.get_barrier_semaphore()
    for step in range(1, n_col):
        pl.semaphore_signal(
            barrier, inc=1, device_id={"col": col_peer(step)},
            device_id_type=pl.DeviceIdType.MESH,
        )
    for step in range(lanes, planes):
        away = lax.rem(mem * lanes + step, planes)
        pl.semaphore_signal(
            barrier, inc=1, device_id=in_plane(away), device_id_type=pl.DeviceIdType.MESH
        )
    pl.semaphore_wait(barrier, n_col - 1 + planes - lanes)

    each(1, rows, lambda step: inc_copy(step).start())
    each(0, ahead, send_chunk)
    incr[plane, row] = inc[...]
    reach_rows = jnp.broadcast_to(reach[...].astype(jnp.float32), (width, levels)).T
    for s in range(slots):
        active[s] = jnp.where(reach_rows > float(s), 1.0, 0.0).astype(jnp.bfloat16)
    root_load.wait()
    for v in range(variables):
        root_t[v] = root[v].astype(jnp.float32).T.astype(jnp.bfloat16)

    def clear(v):
        for p in range(planes):
            total[v, p] = jnp.zeros(total.shape[2:], jnp.float32)

    each(0, variables, clear)
    tiles_load.wait()
    each(1, rows, lambda step: inc_arrival(step).wait_recv())
    each(1, planes, lambda step: inc2_copy(step).start())
    each(1, planes, lambda step: inc2_arrival(step).wait_recv())

    def finish_levels(v):
        each(1, planes, lambda step: part_arrival(v, step).wait_recv())

        def block(b):
            summed = total[v, plane, b]
            for step in range(1, planes):
                summed += part_in[v, plane_peer(step), b].astype(jnp.float32)
            total[v, plane, b] = summed
            line_out[v, b] = summed.astype(jnp.bfloat16)

        each(0, rows, block)
        each(1, rows, lambda step: line_copy(v, step).start())

    def chunk_step(chunk):
        v, half = chunk // halves, lax.rem(chunk, halves)
        own_copy(chunk).wait()
        each(1, n_col, lambda step: member_arrival(chunk, step).wait_recv())

        @pl.when(chunk + ahead < chunks)
        def _():
            send_chunk(chunk + ahead)

        def lift(b):
            field = jnp.concatenate(
                [incr[p * lanes + lax.rem(b, lanes), b // lanes, v] for p in range(n_mem)], 0
            ).astype(jnp.float32)
            weighted = jnp.concatenate(
                [
                    (recv[chunk, b, i].astype(jnp.float32) * field).astype(jnp.bfloat16)
                    for i in range(group)
                ],
                1,
            )
            lifted = jnp.dot(
                root_t[v], weighted, preferred_element_type=jnp.float32
            ).astype(jnp.bfloat16)
            for i in range(group):
                grid[b, i] = lifted[:, i * width:(i + 1) * width]

        together(lift)

        def spread(r):
            picked = jnp.concatenate(
                [grid[slot_block[r, s]] * active[s][None] for s in range(slots)], 2
            )
            spread_rows = jnp.dot(
                picked.reshape(group * levels, slots * width), tiles[r],
                preferred_element_type=jnp.float32,
            ).astype(jnp.bfloat16)
            side = jnp.concatenate(
                [spread_rows[i * levels:(i + 1) * levels] for i in range(group)], 1
            )
            lowered = jnp.dot(root[v], side, preferred_element_type=jnp.float32)
            summed = recv[chunk, r, 0].astype(jnp.float32) * lowered[:, :width]
            for i in range(1, group):
                summed += (
                    recv[chunk, r, i].astype(jnp.float32) * lowered[:, i * width:(i + 1) * width]
                )
            for p in range(n_mem):
                total[v, p * lanes + lax.rem(r, lanes), r // lanes] += summed[p * quarter:(p + 1) * quarter]

        together(spread)

        @pl.when(half == halves - 1)
        def _():
            for p in range(planes):
                part_out[v, p] = total[v, p].astype(jnp.bfloat16)
            each(1, planes, lambda step: part_copy(v, step).start())

        @pl.when((half == 0) & (v > 0))
        def _():
            finish_levels(v - 1)

    each(0, chunks, chunk_step)
    finish_levels(variables - 1)

    for v in range(variables):
        each(1, rows, lambda step: line_arrival(v, step).wait_recv())
        summed = total[v, plane, row]
        for step in range(1, rows):
            summed += line_in[v, row_peer(step)].astype(jnp.float32)
        out[v] = (summed / scale).astype(out.dtype)

    each(1, rows, lambda step: inc_copy(step).wait_send())
    each(1, planes, lambda step: inc2_copy(step).wait_send())
    each(0, chunks, lambda chunk: each(
        1, n_col, lambda step: member_copy(chunk, step).wait_send()))
    each(0, variables, lambda v: each(
        1, planes, lambda step: part_copy(v, step).wait_send()))
    each(0, variables, lambda v: each(
        1, rows, lambda step: line_copy(v, step).wait_send()))


def on_device(ensemble, increment, vert_root, tiles, tile_col, level_reach):
    n_mem, n_col = lax.axis_size("mem"), lax.axis_size("col")
    members, variables, levels, width = ensemble.shape
    n_blocks, slots = tiles.shape[:2]
    per_device = members // n_col
    halves = per_device // 2 if per_device % 4 == 0 else 2 - per_device % 2
    group = per_device // halves
    chunks = variables * halves
    quarter = levels // n_mem
    lanes = 2 if n_col % 2 == 0 else 1
    rows, planes = n_col // lanes, n_mem * lanes
    dma = pltpu.SemaphoreType.DMA
    vmem = pl.BlockSpec(memory_space=pltpu.VMEM)
    bf16 = jnp.bfloat16
    return pl.pallas_call(
        functools.partial(kernel, n_mem, n_col, halves, float(members * n_mem - 1)),
        out_shape=jax.ShapeDtypeStruct(increment.shape, bf16),
        in_specs=[
            pl.BlockSpec(memory_space=pltpu.SMEM),
            pl.BlockSpec(memory_space=pl.ANY),
            vmem, pl.BlockSpec(memory_space=pl.ANY), pl.BlockSpec(memory_space=pl.ANY), vmem,
        ],
        out_specs=vmem,
        scratch_shapes=[
            pltpu.VMEM(vert_root.shape, bf16),
            pltpu.VMEM(vert_root.shape, bf16),
            pltpu.VMEM((n_blocks, slots * width, width), bf16),
            pltpu.VMEM((slots, levels, width), bf16),
            dma((2,)),
            pltpu.VMEM((chunks, n_col, group, levels, width), bf16),
            pltpu.VMEM((planes, rows, variables, quarter, width), bf16),
            pltpu.VMEM((n_col, group, levels, width), bf16),
            pltpu.VMEM((variables, planes, rows, quarter, width), jnp.float32),
            pltpu.VMEM((variables, planes, rows, quarter, width), bf16),
            pltpu.VMEM((variables, planes, rows, quarter, width), bf16),
            pltpu.VMEM((variables, rows, quarter, width), bf16),
            pltpu.VMEM((variables, rows, quarter, width), bf16),
            dma((chunks, n_col)),
            dma((chunks, n_col)),
            dma((chunks,)),
            dma((rows,)),
            dma((rows,)),
            dma((planes,)),
            dma((planes,)),
            dma((variables, planes)),
            dma((variables, planes)),
            dma((variables, rows)),
            dma((variables, rows)),
        ],
        compiler_params=pltpu.CompilerParams(
            collective_id=0, has_side_effects=True, vmem_limit_bytes=56 * 1024 * 1024
        ),
        name="localized_covariance",
    )(
        tile_col, ensemble, increment, vert_root,
        tiles.reshape(n_blocks, slots * width, width), level_reach.reshape(1, levels),
    )


def solution(mesh):
    placed = (P("mem", None, None, "col"), P(None, "mem", "col"), P(), P(), P(), P())
    return jax.shard_map(
        on_device, mesh=mesh, in_specs=placed, out_specs=P(None, "mem", "col"), check_vma=False
    )
```

```python
import functools

import jax
import jax.numpy as jnp
from jax import lax
from jax.experimental import pallas as pl
from jax.experimental.pallas import tpu as pltpu
from jax.sharding import PartitionSpec as P


def kernel(
    n_mem, n_col, halves, parts, scale,
    slot_block, ens, inc, root_in, tiles_in, reach, out,
    root, root_t, tiles, active, load_sem, recv, incr, grid, total, part_out, part_in, line_out, line_in,
    send_sem, recv_sem, own_sem, inc_send, inc_recv, inc2_send, inc2_recv,
    part_send, part_recv, line_send, line_recv,
):
    mem, col = lax.axis_index("mem"), lax.axis_index("col")
    variables, levels, width = ens.shape[1], ens.shape[2], ens.shape[3]
    per_device = ens.shape[0] // n_col
    group = per_device // halves
    quarter = levels // n_mem
    slots = active.shape[0]
    chunks = variables * halves
    ahead = min(3, chunks)
    side_by_side = 4 if n_col % 4 == 0 else 1

    def col_peer(step):
        return lax.rem(col + step, n_col)

    lanes = 2 if n_col % 2 == 0 else 1
    rows, planes = n_col // lanes, n_mem * lanes
    lane, row = lax.rem(col, lanes), col // lanes
    plane = mem * lanes + lane
    span = rows // parts

    def row_peer(step):
        return lax.rem(row + step, rows)

    def plane_peer(step):
        return lax.rem(plane + step, planes)

    def in_row(peer):
        return {"col": peer * lanes + lane}

    def in_plane(peer):
        return {"mem": peer // lanes, "col": row * lanes + lax.rem(peer, lanes)}

    def each(low, high, body):
        def step(index, carry):
            body(index)
            return carry
        lax.fori_loop(low, high, step, 0)

    def together(low, high, body):
        def step(index):
            for k in range(side_by_side):
                body(index * side_by_side + k)
        each(low, high, step)

    def remote(src, dst, send, receive, peer):
        return pltpu.make_async_remote_copy(
            src_ref=src, dst_ref=dst, send_sem=send, recv_sem=receive,
            device_id=peer, device_id_type=pl.DeviceIdType.MESH,
        )

    def far_first(k):
        return n_col // 2 + (k // 2) * (1 - 2 * lax.rem(k, 2))

    def members_of(owner, chunk):
        first = owner * per_device + lax.rem(chunk, halves) * group
        return ens.at[pl.ds(first, group), chunk // halves]

    def member_copy(chunk, step):
        peer = col_peer(step)
        return remote(
            members_of(peer, chunk), recv.at[chunk, col],
            send_sem.at[chunk, peer], recv_sem.at[chunk, col], {"col": peer},
        )

    def member_arrival(chunk, step):
        peer = col_peer(step)
        return remote(
            members_of(peer, chunk), recv.at[chunk, peer],
            send_sem.at[chunk, peer], recv_sem.at[chunk, peer], {"col": peer},
        )

    def own_copy(chunk):
        return pltpu.make_async_copy(
            members_of(col, chunk), recv.at[chunk, col], own_sem.at[chunk]
        )

    def send_chunk(chunk):
        own_copy(chunk).start()
        each(1, n_col, lambda k: member_copy(chunk, far_first(k)).start())

    def inc_copy(step):
        peer = row_peer(step)
        return remote(inc, incr.at[plane, row], inc_send.at[peer], inc_recv.at[row], in_row(peer))

    def inc_arrival(step):
        peer = row_peer(step)
        return remote(inc, incr.at[plane, peer], inc_send.at[peer], inc_recv.at[peer], in_row(peer))

    def inc2_copy(step):
        peer = plane_peer(step)
        return remote(
            incr.at[plane], incr.at[plane], inc2_send.at[peer], inc2_recv.at[plane],
            in_plane(peer),
        )

    def inc2_arrival(step):
        peer = plane_peer(step)
        return remote(
            incr.at[peer], incr.at[peer], inc2_send.at[peer], inc2_recv.at[peer],
            in_plane(peer),
        )

    def part_copy(v, part, step):
        peer, blocks = plane_peer(step), pl.ds(part * span, span)
        return remote(
            part_out.at[v, peer, blocks], part_in.at[v, plane, blocks],
            part_send.at[v * parts + part, peer], part_recv.at[v * parts + part, plane],
            in_plane(peer),
        )

    def part_arrival(v, part, step):
        peer, blocks = plane_peer(step), pl.ds(part * span, span)
        return remote(
            part_out.at[v, peer, blocks], part_in.at[v, peer, blocks],
            part_send.at[v * parts + part, peer], part_recv.at[v * parts + part, peer],
            in_plane(peer),
        )

    def line_copy(v, step):
        peer = row_peer(step)
        return remote(
            line_out.at[v, peer], line_in.at[v, row],
            line_send.at[v, peer], line_recv.at[v, row], in_row(peer),
        )

    def line_arrival(v, step):
        peer = row_peer(step)
        return remote(
            line_out.at[v, peer], line_in.at[v, peer],
            line_send.at[v, peer], line_recv.at[v, peer], in_row(peer),
        )

    root_load = pltpu.make_async_copy(root_in, root, load_sem.at[0])
    tiles_load = pltpu.make_async_copy(tiles_in, tiles, load_sem.at[1])
    root_load.start()
    tiles_load.start()

    barrier = pltpu.get_barrier_semaphore()
    for step in range(1, n_col):
        pl.semaphore_signal(
            barrier, inc=1, device_id={"col": col_peer(step)},
            device_id_type=pl.DeviceIdType.MESH,
        )
    for step in range(lanes, planes):
        away = lax.rem(mem * lanes + step, planes)
        pl.semaphore_signal(
            barrier, inc=1, device_id=in_plane(away), device_id_type=pl.DeviceIdType.MESH
        )
    pl.semaphore_wait(barrier, n_col - 1 + planes - lanes)

    each(1, rows, lambda step: inc_copy(step).start())
    each(0, ahead, send_chunk)
    incr[plane, row] = inc[...]
    reach_rows = jnp.broadcast_to(reach[...].astype(jnp.float32), (width, levels)).T
    for s in range(slots):
        active[s] = jnp.where(reach_rows > float(s), 1.0, 0.0).astype(jnp.bfloat16)
    root_load.wait()
    for v in range(variables):
        root_t[v] = root[v].astype(jnp.float32).T.astype(jnp.bfloat16)

    def clear(v):
        for p in range(planes):
            total[v, p] = jnp.zeros(total.shape[2:], jnp.float32)

    each(0, variables, clear)
    tiles_load.wait()
    each(1, rows, lambda step: inc_arrival(step).wait_recv())
    each(1, planes, lambda step: inc2_copy(step).start())
    each(1, planes, lambda step: inc2_arrival(step).wait_recv())

    def finish_levels(v):
        for part in range(parts):
            each(1, planes, lambda step: part_arrival(v, part, step).wait_recv())

        def block(b):
            summed = total[v, plane, b]
            for step in range(1, planes):
                summed += part_in[v, plane_peer(step), b].astype(jnp.float32)
            total[v, plane, b] = summed
            line_out[v, b] = summed.astype(jnp.bfloat16)

        each(0, rows, block)
        each(1, rows, lambda step: line_copy(v, step).start())

    def chunk_step(chunk):
        v, half = chunk // halves, lax.rem(chunk, halves)
        own_copy(chunk).wait()

        def lift(b):
            field = jnp.concatenate(
                [incr[p * lanes + lax.rem(b, lanes), b // lanes, v] for p in range(n_mem)], 0
            ).astype(jnp.float32)
            weighted = jnp.concatenate(
                [
                    (recv[chunk, b, i].astype(jnp.float32) * field).astype(jnp.bfloat16)
                    for i in range(group)
                ],
                1,
            )
            lifted = jnp.dot(
                root_t[v], weighted, preferred_element_type=jnp.float32
            ).astype(jnp.bfloat16)
            for i in range(group):
                grid[b, i] = lifted[:, i * width:(i + 1) * width]

        def lift_group(index):
            order = [index * side_by_side + k for k in range(side_by_side)]
            for place in order:

                @pl.when(place > 0)
                def _():
                    member_arrival(chunk, far_first(n_col - place)).wait_recv()

            for place in order:
                lift(col_peer(far_first(n_col - place)))

        each(0, n_col // side_by_side, lift_group)

        @pl.when(chunk + ahead < chunks)
        def _():
            send_chunk(chunk + ahead)

        def spread(r):
            picked = jnp.concatenate(
                [grid[slot_block[r, s]] * active[s][None] for s in range(slots)], 2
            )
            spread_rows = jnp.dot(
                picked.reshape(group * levels, slots * width), tiles[r],
                preferred_element_type=jnp.float32,
            ).astype(jnp.bfloat16)
            side = jnp.concatenate(
                [spread_rows[i * levels:(i + 1) * levels] for i in range(group)], 1
            )
            lowered = jnp.dot(root[v], side, preferred_element_type=jnp.float32)
            summed = recv[chunk, r, 0].astype(jnp.float32) * lowered[:, :width]
            for i in range(1, group):
                summed += (
                    recv[chunk, r, i].astype(jnp.float32) * lowered[:, i * width:(i + 1) * width]
                )
            for p in range(n_mem):
                total[v, p * lanes + lax.rem(r, lanes), r // lanes] += summed[p * quarter:(p + 1) * quarter]

        def spread_part(part):
            groups = n_col // side_by_side // parts
            together(part * groups, (part + 1) * groups, spread)

            @pl.when(half == halves - 1)
            def _():
                blocks = pl.ds(part * span, span)
                for p in range(planes):
                    part_out[v, p, blocks] = total[v, p, blocks].astype(jnp.bfloat16)
                each(1, planes, lambda step: part_copy(v, part, step).start())

        each(0, parts, spread_part)

        @pl.when((half == 0) & (v > 0))
        def _():
            finish_levels(v - 1)

    each(0, chunks, chunk_step)
    finish_levels(variables - 1)

    for v in range(variables):
        each(1, rows, lambda step: line_arrival(v, step).wait_recv())
        summed = total[v, plane, row]
        for step in range(1, rows):
            summed += line_in[v, row_peer(step)].astype(jnp.float32)
        out[v] = (summed / scale).astype(out.dtype)

    each(1, rows, lambda step: inc_copy(step).wait_send())
    each(1, planes, lambda step: inc2_copy(step).wait_send())
    each(0, chunks, lambda chunk: each(
        1, n_col, lambda step: member_copy(chunk, step).wait_send()))
    each(0, variables, lambda v: each(
        1, planes, lambda step: [part_copy(v, part, step).wait_send() for part in range(parts)]))
    each(0, variables, lambda v: each(
        1, rows, lambda step: line_copy(v, step).wait_send()))


def on_device(ensemble, increment, vert_root, tiles, tile_col, level_reach):
    n_mem, n_col = lax.axis_size("mem"), lax.axis_size("col")
    members, variables, levels, width = ensemble.shape
    n_blocks, slots = tiles.shape[:2]
    per_device = members // n_col
    halves = per_device // 2 if per_device % 4 == 0 else 2 - per_device % 2
    group = per_device // halves
    chunks = variables * halves
    quarter = levels // n_mem
    lanes = 2 if n_col % 2 == 0 else 1
    rows, planes = n_col // lanes, n_mem * lanes
    parts = 2 if n_col % 8 == 0 else 1
    dma = pltpu.SemaphoreType.DMA
    vmem = pl.BlockSpec(memory_space=pltpu.VMEM)
    bf16 = jnp.bfloat16
    return pl.pallas_call(
        functools.partial(kernel, n_mem, n_col, halves, parts, float(members * n_mem - 1)),
        out_shape=jax.ShapeDtypeStruct(increment.shape, bf16),
        in_specs=[
            pl.BlockSpec(memory_space=pltpu.SMEM),
            pl.BlockSpec(memory_space=pl.ANY),
            vmem, pl.BlockSpec(memory_space=pl.ANY), pl.BlockSpec(memory_space=pl.ANY), vmem,
        ],
        out_specs=vmem,
        scratch_shapes=[
            pltpu.VMEM(vert_root.shape, bf16),
            pltpu.VMEM(vert_root.shape, bf16),
            pltpu.VMEM((n_blocks, slots * width, width), bf16),
            pltpu.VMEM((slots, levels, width), bf16),
            dma((2,)),
            pltpu.VMEM((chunks, n_col, group, levels, width), bf16),
            pltpu.VMEM((planes, rows, variables, quarter, width), bf16),
            pltpu.VMEM((n_col, group, levels, width), bf16),
            pltpu.VMEM((variables, planes, rows, quarter, width), jnp.float32),
            pltpu.VMEM((variables, planes, rows, quarter, width), bf16),
            pltpu.VMEM((variables, planes, rows, quarter, width), bf16),
            pltpu.VMEM((variables, rows, quarter, width), bf16),
            pltpu.VMEM((variables, rows, quarter, width), bf16),
            dma((chunks, n_col)),
            dma((chunks, n_col)),
            dma((chunks,)),
            dma((rows,)),
            dma((rows,)),
            dma((planes,)),
            dma((planes,)),
            dma((variables * parts, planes)),
            dma((variables * parts, planes)),
            dma((variables, rows)),
            dma((variables, rows)),
        ],
        compiler_params=pltpu.CompilerParams(
            collective_id=0, has_side_effects=True, vmem_limit_bytes=56 * 1024 * 1024
        ),
        name="localized_covariance",
    )(
        tile_col, ensemble, increment, vert_root,
        tiles.reshape(n_blocks, slots * width, width), level_reach.reshape(1, levels),
    )


def solution(mesh):
    placed = (P("mem", None, None, "col"), P(None, "mem", "col"), P(), P(), P(), P())
    return jax.shard_map(
        on_device, mesh=mesh, in_specs=placed, out_specs=P(None, "mem", "col"), check_vma=False
    )
```

```python
import functools

import jax
import jax.numpy as jnp
from jax import lax
from jax.experimental import pallas as pl
from jax.experimental.pallas import tpu as pltpu
from jax.sharding import PartitionSpec as P


def kernel(
    n_mem, n_col, halves, parts, scale,
    slot_block, ens, inc, root_in, tiles_in, reach, out,
    root, root_t, tiles, active, load_sem, recv, incr, grid, total, part_out, part_in, line_out, line_in,
    send_sem, recv_sem, own_sem, inc_send, inc_recv, inc2_send, inc2_recv,
    part_send, part_recv, line_send, line_recv,
):
    mem, col = lax.axis_index("mem"), lax.axis_index("col")
    variables, levels, width = ens.shape[1], ens.shape[2], ens.shape[3]
    per_device = ens.shape[0] // n_col
    group = per_device // halves
    quarter = levels // n_mem
    slots = active.shape[0]
    chunks = variables * halves
    ahead = min(2, chunks)
    side_by_side = 4 if n_col % 4 == 0 else 1

    def col_peer(step):
        return lax.rem(col + step, n_col)

    lanes = 2 if n_col % 2 == 0 else 1
    rows, planes = n_col // lanes, n_mem * lanes
    lane, row = lax.rem(col, lanes), col // lanes
    plane = mem * lanes + lane
    span = rows // parts

    def row_peer(step):
        return lax.rem(row + step, rows)

    def plane_peer(step):
        return lax.rem(plane + step, planes)

    def in_row(peer):
        return {"col": peer * lanes + lane}

    def in_plane(peer):
        return {"mem": peer // lanes, "col": row * lanes + lax.rem(peer, lanes)}

    def each(low, high, body):
        def step(index, carry):
            body(index)
            return carry
        lax.fori_loop(low, high, step, 0)

    def together(low, high, body):
        def step(index):
            for k in range(side_by_side):
                body(index * side_by_side + k)
        each(low, high, step)

    def remote(src, dst, send, receive, peer):
        return pltpu.make_async_remote_copy(
            src_ref=src, dst_ref=dst, send_sem=send, recv_sem=receive,
            device_id=peer, device_id_type=pl.DeviceIdType.MESH,
        )

    def far_first(k):
        return n_col // 2 + (k // 2) * (1 - 2 * lax.rem(k, 2))

    def members_of(owner, chunk):
        first = owner * per_device + lax.rem(chunk, halves) * group
        return ens.at[pl.ds(first, group), chunk // halves]

    def member_copy(chunk, step):
        peer = col_peer(step)
        return remote(
            members_of(peer, chunk), recv.at[chunk, col],
            send_sem.at[chunk, peer], recv_sem.at[chunk, col], {"col": peer},
        )

    def member_arrival(chunk, step):
        peer = col_peer(step)
        return remote(
            members_of(peer, chunk), recv.at[chunk, peer],
            send_sem.at[chunk, peer], recv_sem.at[chunk, peer], {"col": peer},
        )

    def own_copy(chunk):
        return pltpu.make_async_copy(
            members_of(col, chunk), recv.at[chunk, col], own_sem.at[chunk]
        )

    def send_chunk(chunk):
        own_copy(chunk).start()
        each(1, n_col, lambda k: member_copy(chunk, far_first(k)).start())

    def inc_copy(step):
        peer = row_peer(step)
        return remote(inc, incr.at[plane, row], inc_send.at[peer], inc_recv.at[row], in_row(peer))

    def inc_arrival(step):
        peer = row_peer(step)
        return remote(inc, incr.at[plane, peer], inc_send.at[peer], inc_recv.at[peer], in_row(peer))

    def inc2_copy(step):
        peer = plane_peer(step)
        return remote(
            incr.at[plane], incr.at[plane], inc2_send.at[peer], inc2_recv.at[plane],
            in_plane(peer),
        )

    def inc2_arrival(step):
        peer = plane_peer(step)
        return remote(
            incr.at[peer], incr.at[peer], inc2_send.at[peer], inc2_recv.at[peer],
            in_plane(peer),
        )

    def part_copy(v, part, step):
        peer, blocks = plane_peer(step), pl.ds(part * span, span)
        return remote(
            part_out.at[v, peer, blocks], part_in.at[v, plane, blocks],
            part_send.at[v * parts + part, peer], part_recv.at[v * parts + part, plane],
            in_plane(peer),
        )

    def part_arrival(v, part, step):
        peer, blocks = plane_peer(step), pl.ds(part * span, span)
        return remote(
            part_out.at[v, peer, blocks], part_in.at[v, peer, blocks],
            part_send.at[v * parts + part, peer], part_recv.at[v * parts + part, peer],
            in_plane(peer),
        )

    def line_copy(v, step):
        peer = row_peer(step)
        return remote(
            line_out.at[v, peer], line_in.at[v, row],
            line_send.at[v, peer], line_recv.at[v, row], in_row(peer),
        )

    def line_arrival(v, step):
        peer = row_peer(step)
        return remote(
            line_out.at[v, peer], line_in.at[v, peer],
            line_send.at[v, peer], line_recv.at[v, peer], in_row(peer),
        )

    root_load = pltpu.make_async_copy(root_in, root, load_sem.at[0])
    tiles_load = pltpu.make_async_copy(tiles_in, tiles, load_sem.at[1])
    root_load.start()
    tiles_load.start()

    barrier = pltpu.get_barrier_semaphore()
    for step in range(1, n_col):
        pl.semaphore_signal(
            barrier, inc=1, device_id={"col": col_peer(step)},
            device_id_type=pl.DeviceIdType.MESH,
        )
    for step in range(lanes, planes):
        away = lax.rem(mem * lanes + step, planes)
        pl.semaphore_signal(
            barrier, inc=1, device_id=in_plane(away), device_id_type=pl.DeviceIdType.MESH
        )
    pl.semaphore_wait(barrier, n_col - 1 + planes - lanes)

    each(1, rows, lambda step: inc_copy(step).start())
    each(0, ahead, send_chunk)
    incr[plane, row] = inc[...]
    reach_rows = jnp.broadcast_to(reach[...].astype(jnp.float32), (width, levels)).T
    for s in range(slots):
        active[s] = jnp.where(reach_rows > float(s), 1.0, 0.0).astype(jnp.bfloat16)
    root_load.wait()
    for v in range(variables):
        root_t[v] = root[v].astype(jnp.float32).T.astype(jnp.bfloat16)

    def clear(v):
        for p in range(planes):
            total[v, p] = jnp.zeros(total.shape[2:], jnp.float32)

    each(0, variables, clear)
    tiles_load.wait()
    each(1, rows, lambda step: inc_arrival(step).wait_recv())
    each(1, planes, lambda step: inc2_copy(step).start())
    each(1, planes, lambda step: inc2_arrival(step).wait_recv())

    def finish_levels(v):
        for part in range(parts):
            each(1, planes, lambda step: part_arrival(v, part, step).wait_recv())

        def block(b):
            summed = total[v, plane, b]
            for step in range(1, planes):
                summed += part_in[v, plane_peer(step), b].astype(jnp.float32)
            total[v, plane, b] = summed
            line_out[v, b] = summed.astype(jnp.bfloat16)

        each(0, rows, block)
        each(1, rows, lambda step: line_copy(v, step).start())

    def chunk_step(chunk):
        v, half = chunk // halves, lax.rem(chunk, halves)
        own_copy(chunk).wait()

        def lift(b):
            field = jnp.concatenate(
                [incr[p * lanes + lax.rem(b, lanes), b // lanes, v] for p in range(n_mem)], 0
            ).astype(jnp.float32)
            weighted = jnp.concatenate(
                [
                    (recv[chunk, b, i].astype(jnp.float32) * field).astype(jnp.bfloat16)
                    for i in range(group)
                ],
                1,
            )
            lifted = jnp.dot(
                root_t[v], weighted, preferred_element_type=jnp.float32
            ).astype(jnp.bfloat16)
            for i in range(group):
                grid[b, i] = lifted[:, i * width:(i + 1) * width]

        def lift_group(index):
            order = [index * side_by_side + k for k in range(side_by_side)]
            for place in order:

                @pl.when(place > 0)
                def _():
                    member_arrival(chunk, far_first(n_col - place)).wait_recv()

            for place in order:
                lift(col_peer(far_first(n_col - place)))

        each(0, n_col // side_by_side, lift_group)

        @pl.when(chunk + ahead < chunks)
        def _():
            send_chunk(chunk + ahead)

        def spread(r):
            picked = jnp.concatenate(
                [grid[slot_block[r, s]] * active[s][None] for s in range(slots)], 2
            )
            spread_rows = jnp.dot(
                picked.reshape(group * levels, slots * width), tiles[r],
                preferred_element_type=jnp.float32,
            ).astype(jnp.bfloat16)
            side = jnp.concatenate(
                [spread_rows[i * levels:(i + 1) * levels] for i in range(group)], 1
            )
            lowered = jnp.dot(root[v], side, preferred_element_type=jnp.float32)
            summed = recv[chunk, r, 0].astype(jnp.float32) * lowered[:, :width]
            for i in range(1, group):
                summed += (
                    recv[chunk, r, i].astype(jnp.float32) * lowered[:, i * width:(i + 1) * width]
                )
            for p in range(n_mem):
                total[v, p * lanes + lax.rem(r, lanes), r // lanes] += summed[p * quarter:(p + 1) * quarter]

        def spread_part(part):
            groups = n_col // side_by_side // parts
            together(part * groups, (part + 1) * groups, spread)

            @pl.when(half == halves - 1)
            def _():
                blocks = pl.ds(part * span, span)
                for p in range(planes):
                    part_out[v, p, blocks] = total[v, p, blocks].astype(jnp.bfloat16)
                each(1, planes, lambda step: part_copy(v, part, step).start())

        each(0, parts, spread_part)

        @pl.when((half == 0) & (v > 0))
        def _():
            finish_levels(v - 1)

    each(0, chunks, chunk_step)
    finish_levels(variables - 1)

    for v in range(variables):
        each(1, rows, lambda step: line_arrival(v, step).wait_recv())
        summed = total[v, plane, row]
        for step in range(1, rows):
            summed += line_in[v, row_peer(step)].astype(jnp.float32)
        out[v] = (summed / scale).astype(out.dtype)

    each(1, rows, lambda step: inc_copy(step).wait_send())
    each(1, planes, lambda step: inc2_copy(step).wait_send())
    each(0, chunks, lambda chunk: each(
        1, n_col, lambda step: member_copy(chunk, step).wait_send()))
    each(0, variables, lambda v: each(
        1, planes, lambda step: [part_copy(v, part, step).wait_send() for part in range(parts)]))
    each(0, variables, lambda v: each(
        1, rows, lambda step: line_copy(v, step).wait_send()))


def on_device(ensemble, increment, vert_root, tiles, tile_col, level_reach):
    n_mem, n_col = lax.axis_size("mem"), lax.axis_size("col")
    members, variables, levels, width = ensemble.shape
    n_blocks, slots = tiles.shape[:2]
    per_device = members // n_col
    halves = per_device // 2 if per_device % 4 == 0 else 2 - per_device % 2
    group = per_device // halves
    chunks = variables * halves
    quarter = levels // n_mem
    lanes = 2 if n_col % 2 == 0 else 1
    rows, planes = n_col // lanes, n_mem * lanes
    parts = 2 if n_col % 8 == 0 else 1
    dma = pltpu.SemaphoreType.DMA
    vmem = pl.BlockSpec(memory_space=pltpu.VMEM)
    bf16 = jnp.bfloat16
    return pl.pallas_call(
        functools.partial(kernel, n_mem, n_col, halves, parts, float(members * n_mem - 1)),
        out_shape=jax.ShapeDtypeStruct(increment.shape, bf16),
        in_specs=[
            pl.BlockSpec(memory_space=pltpu.SMEM),
            pl.BlockSpec(memory_space=pl.ANY),
            vmem, pl.BlockSpec(memory_space=pl.ANY), pl.BlockSpec(memory_space=pl.ANY), vmem,
        ],
        out_specs=vmem,
        scratch_shapes=[
            pltpu.VMEM(vert_root.shape, bf16),
            pltpu.VMEM(vert_root.shape, bf16),
            pltpu.VMEM((n_blocks, slots * width, width), bf16),
            pltpu.VMEM((slots, levels, width), bf16),
            dma((2,)),
            pltpu.VMEM((chunks, n_col, group, levels, width), bf16),
            pltpu.VMEM((planes, rows, variables, quarter, width), bf16),
            pltpu.VMEM((n_col, group, levels, width), bf16),
            pltpu.VMEM((variables, planes, rows, quarter, width), jnp.float32),
            pltpu.VMEM((variables, planes, rows, quarter, width), bf16),
            pltpu.VMEM((variables, planes, rows, quarter, width), bf16),
            pltpu.VMEM((variables, rows, quarter, width), bf16),
            pltpu.VMEM((variables, rows, quarter, width), bf16),
            dma((chunks, n_col)),
            dma((chunks, n_col)),
            dma((chunks,)),
            dma((rows,)),
            dma((rows,)),
            dma((planes,)),
            dma((planes,)),
            dma((variables * parts, planes)),
            dma((variables * parts, planes)),
            dma((variables, rows)),
            dma((variables, rows)),
        ],
        compiler_params=pltpu.CompilerParams(
            collective_id=0, has_side_effects=True, vmem_limit_bytes=56 * 1024 * 1024
        ),
        name="localized_covariance",
    )(
        tile_col, ensemble, increment, vert_root,
        tiles.reshape(n_blocks, slots * width, width), level_reach.reshape(1, levels),
    )


def solution(mesh):
    placed = (P("mem", None, None, "col"), P(None, "mem", "col"), P(), P(), P(), P())
    return jax.shard_map(
        on_device, mesh=mesh, in_specs=placed, out_specs=P(None, "mem", "col"), check_vma=False
    )
```

```python
import functools

import jax
import jax.numpy as jnp
from jax import lax
from jax.experimental import pallas as pl
from jax.experimental.pallas import tpu as pltpu
from jax.sharding import PartitionSpec as P


def kernel(
    n_mem, n_col, halves, parts, scale,
    slot_block, ens, inc, root_in, tiles_in, reach, out,
    root, root_t, tiles, active, load_sem, recv, incr, grid, total, part_out, part_in, line_out, line_in,
    send_sem, recv_sem, own_sem, inc_send, inc_recv, inc2_send, inc2_recv,
    part_send, part_recv, line_send, line_recv,
):
    mem, col = lax.axis_index("mem"), lax.axis_index("col")
    variables, levels, width = ens.shape[1], ens.shape[2], ens.shape[3]
    per_device = ens.shape[0] // n_col
    group = per_device // halves
    quarter = levels // n_mem
    slots = active.shape[0]
    chunks = variables * halves
    ahead = min(2, chunks)
    side_by_side = 4 if n_col % 4 == 0 else 1

    def col_peer(step):
        return lax.rem(col + step, n_col)

    lanes = 2 if n_col % 2 == 0 else 1
    rows, planes = n_col // lanes, n_mem * lanes
    lane, row = lax.rem(col, lanes), col // lanes
    plane = mem * lanes + lane
    span = rows // parts

    def row_peer(step):
        return lax.rem(row + step, rows)

    def plane_peer(step):
        return lax.rem(plane + step, planes)

    def in_row(peer):
        return {"col": peer * lanes + lane}

    def in_plane(peer):
        return {"mem": peer // lanes, "col": row * lanes + lax.rem(peer, lanes)}

    def each(low, high, body):
        def step(index, carry):
            body(index)
            return carry
        lax.fori_loop(low, high, step, 0)

    def together(low, high, body):
        def step(index):
            for k in range(side_by_side):
                body(index * side_by_side + k)
        each(low, high, step)

    def remote(src, dst, send, receive, peer):
        return pltpu.make_async_remote_copy(
            src_ref=src, dst_ref=dst, send_sem=send, recv_sem=receive,
            device_id=peer, device_id_type=pl.DeviceIdType.MESH,
        )

    def far_first(k):
        return n_col // 2 + (k // 2) * (1 - 2 * lax.rem(k, 2))

    def members_of(owner, chunk):
        first = owner * per_device + lax.rem(chunk, halves) * group
        return ens.at[pl.ds(first, group), chunk // halves]

    def member_copy(chunk, step):
        peer = col_peer(step)
        return remote(
            members_of(peer, chunk), recv.at[chunk, col],
            send_sem.at[chunk, peer], recv_sem.at[chunk, col], {"col": peer},
        )

    def member_arrival(chunk, step):
        peer = col_peer(step)
        return remote(
            members_of(peer, chunk), recv.at[chunk, peer],
            send_sem.at[chunk, peer], recv_sem.at[chunk, peer], {"col": peer},
        )

    def own_copy(chunk):
        return pltpu.make_async_copy(
            members_of(col, chunk), recv.at[chunk, col], own_sem.at[chunk]
        )

    def send_chunk(chunk):
        own_copy(chunk).start()
        each(1, n_col, lambda k: member_copy(chunk, far_first(k)).start())

    def inc_copy(step):
        peer = row_peer(step)
        return remote(inc, incr.at[plane, row], inc_send.at[peer], inc_recv.at[row], in_row(peer))

    def inc_arrival(step):
        peer = row_peer(step)
        return remote(inc, incr.at[plane, peer], inc_send.at[peer], inc_recv.at[peer], in_row(peer))

    def inc2_copy(step):
        peer = plane_peer(step)
        return remote(
            incr.at[plane], incr.at[plane], inc2_send.at[peer], inc2_recv.at[plane],
            in_plane(peer),
        )

    def inc2_arrival(step):
        peer = plane_peer(step)
        return remote(
            incr.at[peer], incr.at[peer], inc2_send.at[peer], inc2_recv.at[peer],
            in_plane(peer),
        )

    def part_copy(v, part, step):
        peer, blocks = plane_peer(step), pl.ds(part * span, span)
        return remote(
            part_out.at[v, peer, blocks], part_in.at[v, plane, blocks],
            part_send.at[v * parts + part, peer], part_recv.at[v * parts + part, plane],
            in_plane(peer),
        )

    def part_arrival(v, part, step):
        peer, blocks = plane_peer(step), pl.ds(part * span, span)
        return remote(
            part_out.at[v, peer, blocks], part_in.at[v, peer, blocks],
            part_send.at[v * parts + part, peer], part_recv.at[v * parts + part, peer],
            in_plane(peer),
        )

    def line_copy(v, step):
        peer = row_peer(step)
        return remote(
            line_out.at[v, peer], line_in.at[v, row],
            line_send.at[v, peer], line_recv.at[v, row], in_row(peer),
        )

    def line_arrival(v, step):
        peer = row_peer(step)
        return remote(
            line_out.at[v, peer], line_in.at[v, peer],
            line_send.at[v, peer], line_recv.at[v, peer], in_row(peer),
        )

    root_load = pltpu.make_async_copy(root_in, root, load_sem.at[0])
    tiles_load = pltpu.make_async_copy(tiles_in, tiles, load_sem.at[1])
    root_load.start()
    tiles_load.start()

    barrier = pltpu.get_barrier_semaphore()
    for step in range(1, n_col):
        pl.semaphore_signal(
            barrier, inc=1, device_id={"col": col_peer(step)},
            device_id_type=pl.DeviceIdType.MESH,
        )
    for step in range(lanes, planes):
        away = lax.rem(mem * lanes + step, planes)
        pl.semaphore_signal(
            barrier, inc=1, device_id=in_plane(away), device_id_type=pl.DeviceIdType.MESH
        )
    pl.semaphore_wait(barrier, n_col - 1 + planes - lanes)

    each(1, rows, lambda step: inc_copy(step).start())
    each(0, ahead, send_chunk)
    incr[plane, row] = inc[...]
    reach_rows = jnp.broadcast_to(reach[...].astype(jnp.float32), (width, levels)).T
    for s in range(slots):
        active[s] = jnp.where(reach_rows > float(s), 1.0, 0.0).astype(jnp.bfloat16)
    root_load.wait()
    for v in range(variables):
        root_t[v] = root[v].astype(jnp.float32).T.astype(jnp.bfloat16)

    def clear(v):
        for p in range(planes):
            total[v, p] = jnp.zeros(total.shape[2:], jnp.float32)

    each(0, variables, clear)
    tiles_load.wait()
    each(1, rows, lambda step: inc_arrival(step).wait_recv())
    each(1, planes, lambda step: inc2_copy(step).start())
    each(1, planes, lambda step: inc2_arrival(step).wait_recv())

    def finish_levels(v):
        for part in range(parts):
            each(1, planes, lambda step: part_arrival(v, part, step).wait_recv())

        def block(b):
            summed = total[v, plane, b]
            for step in range(1, planes):
                summed += part_in[v, plane_peer(step), b].astype(jnp.float32)
            total[v, plane, b] = summed
            line_out[v, b] = summed.astype(jnp.bfloat16)

        each(0, rows, block)
        each(1, rows, lambda step: line_copy(v, step).start())

    def chunk_step(chunk):
        v, half = chunk // halves, lax.rem(chunk, halves)
        own_copy(chunk).wait()

        def lift(b):
            field = jnp.concatenate(
                [incr[p * lanes + lax.rem(b, lanes), b // lanes, v] for p in range(n_mem)], 0
            ).astype(jnp.float32)
            weighted = jnp.concatenate(
                [
                    (recv[chunk, b, i].astype(jnp.float32) * field).astype(jnp.bfloat16)
                    for i in range(group)
                ],
                1,
            )
            lifted = jnp.dot(
                root_t[v], weighted, preferred_element_type=jnp.float32
            ).astype(jnp.bfloat16)
            for i in range(group):
                grid[b, i] = lifted[:, i * width:(i + 1) * width]

        def lift_group(index):
            order = [index * side_by_side + k for k in range(side_by_side)]
            for place in order:

                @pl.when(place > 0)
                def _():
                    member_arrival(chunk, far_first(n_col - place)).wait_recv()

            for place in order:
                lift(col_peer(far_first(n_col - place)))

        each(0, n_col // side_by_side, lift_group)

        @pl.when(chunk + ahead < chunks)
        def _():
            send_chunk(chunk + ahead)

        def spread(r):
            picked = jnp.concatenate(
                [grid[slot_block[r, s]] * active[s][None] for s in range(slots)], 2
            )
            spread_rows = jnp.dot(
                picked.reshape(group * levels, slots * width), tiles[r],
                preferred_element_type=jnp.float32,
            ).astype(jnp.bfloat16)
            side = jnp.concatenate(
                [spread_rows[i * levels:(i + 1) * levels] for i in range(group)], 1
            )
            lowered = jnp.dot(root[v], side, preferred_element_type=jnp.float32)
            summed = recv[chunk, r, 0].astype(jnp.float32) * lowered[:, :width]
            for i in range(1, group):
                summed += (
                    recv[chunk, r, i].astype(jnp.float32) * lowered[:, i * width:(i + 1) * width]
                )
            for p in range(n_mem):
                total[v, p * lanes + lax.rem(r, lanes), r // lanes] += summed[p * quarter:(p + 1) * quarter]

        def spread_part(part):
            groups = n_col // side_by_side // parts
            together(part * groups, (part + 1) * groups, spread)

            @pl.when(half == halves - 1)
            def _():
                blocks = pl.ds(part * span, span)
                for p in range(planes):
                    part_out[v, p, blocks] = total[v, p, blocks].astype(jnp.bfloat16)
                each(1, planes, lambda step: part_copy(v, part, step).start())

        each(0, parts, spread_part)

        @pl.when((half == 0) & (v > 0))
        def _():
            finish_levels(v - 1)

    each(0, chunks, chunk_step)
    finish_levels(variables - 1)

    for v in range(variables):
        each(1, rows, lambda step: line_arrival(v, step).wait_recv())
        summed = total[v, plane, row]
        for step in range(1, rows):
            summed += line_in[v, row_peer(step)].astype(jnp.float32)
        out[v] = (summed / scale).astype(out.dtype)

    each(1, rows, lambda step: inc_copy(step).wait_send())
    each(1, planes, lambda step: inc2_copy(step).wait_send())
    each(0, chunks, lambda chunk: each(
        1, n_col, lambda step: member_copy(chunk, step).wait_send()))
    each(0, variables, lambda v: each(
        1, planes, lambda step: [part_copy(v, part, step).wait_send() for part in range(parts)]))
    each(0, variables, lambda v: each(
        1, rows, lambda step: line_copy(v, step).wait_send()))


def on_device(ensemble, increment, vert_root, tiles, tile_col, level_reach):
    n_mem, n_col = lax.axis_size("mem"), lax.axis_size("col")
    members, variables, levels, width = ensemble.shape
    n_blocks, slots = tiles.shape[:2]
    per_device = members // n_col
    halves = 2 - per_device % 2
    group = per_device // halves
    chunks = variables * halves
    quarter = levels // n_mem
    lanes = 2 if n_col % 2 == 0 else 1
    rows, planes = n_col // lanes, n_mem * lanes
    parts = 2 if n_col % 8 == 0 else 1
    dma = pltpu.SemaphoreType.DMA
    vmem = pl.BlockSpec(memory_space=pltpu.VMEM)
    bf16 = jnp.bfloat16
    return pl.pallas_call(
        functools.partial(kernel, n_mem, n_col, halves, parts, float(members * n_mem - 1)),
        out_shape=jax.ShapeDtypeStruct(increment.shape, bf16),
        in_specs=[
            pl.BlockSpec(memory_space=pltpu.SMEM),
            pl.BlockSpec(memory_space=pl.ANY),
            vmem, pl.BlockSpec(memory_space=pl.ANY), pl.BlockSpec(memory_space=pl.ANY), vmem,
        ],
        out_specs=vmem,
        scratch_shapes=[
            pltpu.VMEM(vert_root.shape, bf16),
            pltpu.VMEM(vert_root.shape, bf16),
            pltpu.VMEM((n_blocks, slots * width, width), bf16),
            pltpu.VMEM((slots, levels, width), bf16),
            dma((2,)),
            pltpu.VMEM((chunks, n_col, group, levels, width), bf16),
            pltpu.VMEM((planes, rows, variables, quarter, width), bf16),
            pltpu.VMEM((n_col, group, levels, width), bf16),
            pltpu.VMEM((variables, planes, rows, quarter, width), jnp.float32),
            pltpu.VMEM((variables, planes, rows, quarter, width), bf16),
            pltpu.VMEM((variables, planes, rows, quarter, width), bf16),
            pltpu.VMEM((variables, rows, quarter, width), bf16),
            pltpu.VMEM((variables, rows, quarter, width), bf16),
            dma((chunks, n_col)),
            dma((chunks, n_col)),
            dma((chunks,)),
            dma((rows,)),
            dma((rows,)),
            dma((planes,)),
            dma((planes,)),
            dma((variables * parts, planes)),
            dma((variables * parts, planes)),
            dma((variables, rows)),
            dma((variables, rows)),
        ],
        compiler_params=pltpu.CompilerParams(
            collective_id=0, has_side_effects=True, vmem_limit_bytes=56 * 1024 * 1024
        ),
        name="localized_covariance",
    )(
        tile_col, ensemble, increment, vert_root,
        tiles.reshape(n_blocks, slots * width, width), level_reach.reshape(1, levels),
    )


def solution(mesh):
    placed = (P("mem", None, None, "col"), P(None, "mem", "col"), P(), P(), P(), P())
    return jax.shard_map(
        on_device, mesh=mesh, in_specs=placed, out_specs=P(None, "mem", "col"), check_vma=False
    )
```
